256 devices in a mesh: pb: 16 (over y, z_hi), ha: 8 (over x, z_lo), af: 2 (over core).
Axes of the slice: x: 4, y: 4, z: 8 (z_hi: 4, z_lo: 2; z = z_hi * 2 + z_lo), core: 2. Of those that a mesh axis runs over, the one named last changes fastest.
Arguments:
- queries: bfloat16 [2048, 8192], P('pb', ('ha', 'af')), may hold values from -16 to 16
- vis_keys: bfloat16 [8192, 1024], P(None, 'ha'), may hold values from -16 to 16
- vis_values: bfloat16 [8192, 1024], P(None, 'ha'), may hold values from -6 to 6
- out_grad: bfloat16 [2048, 8192], P('pb', ('ha', 'af')), may hold values from -96 to 96
- key_weight: bfloat16 [8192, 1024], P(None, 'ha'), may hold values from -0.0625 to 0.0625
- value_weight: bfloat16 [8192, 1024], P(None, 'ha'), may hold values from -0.0625 to 0.0625
- frame_ids: int32 [8192], replicated, may hold values from 0 to 7, as said below
- text_mask: int32 [64, 8], P('pb'), may hold values from 0 to 1
Outputs:
- query_grad: bfloat16 [2048, 8192], P('pb', ('ha', 'af'))
- visual_grad: bfloat16 [8192, 8192], P(('pb', 'af'), 'ha')
The draws below stay inside these ranges and needn't reach their ends.
Inputs may be any that keep to these rules, and one draw needn't show every extreme that they name: `frame_ids`: never falls along the visual tokens; every frame holds one token or more, frame 0 two or more.
All inputs are finite; a program needn't handle non-finite values.
Results may differ from the reference program's by a relative error of at most 0.02.
Values may be sent and summed in bfloat16 or wider, within the bound.
No kernel may reach another device: no remote copies, remote signals or barrier semaphores. Data moves between devices by JAX's collectives and lax.ppermute only.
A program may use at most 128 MiB of HBM per device.

```python
import jax
import jax.numpy as jnp
from jax import lax

D = 8192
HQ = 64
KVH = 8
DH = 128
TQ_DEV = 128
VISUAL = 8192
FRAMES = 8
QBLK = 32
TOKENS = 2048


def draw_vis_keys(key, part):
    base_key = jax.random.fold_in(key, 5)
    base = jnp.clip(jax.random.normal(base_key, (VISUAL, KVH * DH), jnp.float32), -6.0, 6.0)
    return base.astype(jnp.bfloat16)


def draw_queries(key, part):
    base_key = jax.random.fold_in(key, 6)
    base = jnp.clip(jax.random.normal(base_key, (TOKENS, HQ * DH), jnp.float32), -6.0, 6.0)
    return base.astype(jnp.bfloat16)


def draw_frame_ids(key, part):
    frame_len = VISUAL // FRAMES
    jitter = jax.random.randint(jax.random.fold_in(key, 11), (FRAMES - 1,), 0, frame_len // 2)
    cuts = (jnp.arange(1, FRAMES) * frame_len + jitter).astype(jnp.int32)
    positions = jnp.arange(VISUAL, dtype=jnp.int32)
    return jnp.sum((positions[:, None] >= cuts[None, :]).astype(jnp.int32), axis=1).astype(jnp.int32)


def draw_text_mask(key, part):
    bits = jax.random.randint(jax.random.fold_in(key, 12), (TOKENS // QBLK, FRAMES), 0, 2)
    return bits.at[:, 0].set(1).astype(jnp.int32)


def block_scale(rng, shape, shards, smallest, largest):
    def one(axis_at, shards_of):
        steps = jax.random.uniform(jax.random.fold_in(jax.random.fold_in(rng, 6), axis_at), (shards_of,), jnp.float32, smallest / len(shards), largest / len(shards))
        return jnp.repeat(jnp.exp(steps), shape[axis_at] // shards_of).reshape((-1,) + (1,) * (len(shape) - axis_at - 1))

    level = one(*shards[0])
    for cut in shards[1:]:
        level = level * one(*cut)
    return level


def gaussian(own_key, extent, scale, reach, pieces=(), kind=jnp.bfloat16):
    drawn = scale * jax.random.normal(own_key, extent, jnp.float32)
    if pieces:
        drawn = drawn * block_scale(own_key, extent, pieces, -0.22, 0.18)
    return jnp.clip(drawn, -reach, reach).astype(kind)


def setup_inputs(seed: int = 0) -> dict:
    arg_keys = jax.random.split(jax.random.key(seed), 9)
    return {
        "queries": draw_queries(jax.random.fold_in(arg_keys[8], 71), 0),
        "vis_keys": draw_vis_keys(jax.random.fold_in(arg_keys[8], 71), 0),
        "vis_values": gaussian(arg_keys[2], (VISUAL, KVH * DH), 1.0, 6.0, ((1, 8),)),
        "out_grad": gaussian(arg_keys[3], (TOKENS, HQ * DH), 16.0, 96.0, ((0, 16), (1, 16))),
        "key_weight": gaussian(arg_keys[4], (D, KVH * DH), D ** -0.5, 0.0625, ((1, 8),)),
        "value_weight": gaussian(arg_keys[5], (D, KVH * DH), D ** -0.5, 0.0625, ((1, 8),)),
        "frame_ids": draw_frame_ids(jax.random.fold_in(arg_keys[8], 71), 0),
        "text_mask": draw_text_mask(jax.random.fold_in(arg_keys[8], 71), 0),
    }


def reference(queries, vis_keys, vis_values, out_grad, key_weight, value_weight, frame_ids, text_mask):
    score_scale = DH ** -0.5
    group_size = HQ // KVH
    tok_count = queries.shape[0]
    blocks = tok_count // TQ_DEV
    onehot = (frame_ids[None, :] == jnp.arange(FRAMES, dtype=jnp.int32)[:, None]).astype(jnp.float32)
    tok_mask = jnp.repeat(text_mask, QBLK, axis=0).astype(jnp.float32)
    allowed = jnp.dot(tok_mask, onehot) > 0.5
    allowed_blocks = allowed.reshape(blocks, TQ_DEV, VISUAL)
    query_cube = queries.reshape(blocks, TQ_DEV, KVH, group_size, DH)
    grad_cube = out_grad.reshape(blocks, TQ_DEV, KVH, group_size, DH)
    query_parts, key_parts, value_parts = [], [], []
    for kv_head in range(KVH):
        key_slab = vis_keys[:, kv_head * DH:(kv_head + 1) * DH].astype(jnp.float32)
        value_slab = vis_values[:, kv_head * DH:(kv_head + 1) * DH].astype(jnp.float32)

        def one_block(totals, inputs):
            query_blk, grad_blk, mask_blk = inputs
            query_wide = query_blk.astype(jnp.float32)
            grad_wide = grad_blk.astype(jnp.float32)
            mask_cube = mask_blk[:, None, :]
            scores = jnp.einsum('thd,vd->thv', query_wide, key_slab) * score_scale
            scores = jnp.where(mask_cube, scores, -1e30)
            row_max = jnp.max(scores, axis=2, keepdims=True)
            numer = jnp.where(mask_cube, jnp.exp(scores - row_max), 0.0)
            attn_prob = numer / jnp.sum(numer, axis=2, keepdims=True)
            prob_low = attn_prob.astype(jnp.bfloat16)
            prob_grad = jnp.einsum('thd,vd->thv', grad_wide, value_slab)
            row_delta = jnp.sum(prob_low.astype(jnp.float32) * prob_grad, axis=2, keepdims=True)
            score_grad = (attn_prob * (prob_grad - row_delta) * score_scale).astype(jnp.bfloat16)
            score_wide = score_grad.astype(jnp.float32)
            query_out = jnp.einsum('thv,vd->thd', score_wide, key_slab).astype(jnp.bfloat16)
            key_total = totals[0] + jnp.einsum('thv,thd->vd', score_wide, query_wide)
            value_total = totals[1] + jnp.einsum('thv,thd->vd', prob_low.astype(jnp.float32), grad_wide)
            return (key_total, value_total), query_out

        start_totals = (jnp.zeros((VISUAL, DH), jnp.float32), jnp.zeros((VISUAL, DH), jnp.float32))
        (key_total, value_total), query_out = lax.scan(one_block, start_totals, (query_cube[:, :, kv_head], grad_cube[:, :, kv_head], allowed_blocks))
        query_parts.append(query_out)
        key_parts.append(key_total.astype(jnp.bfloat16))
        value_parts.append(value_total.astype(jnp.bfloat16))
    query_grad = jnp.stack(query_parts, axis=2).reshape(tok_count, HQ * DH)
    key_grad = jnp.concatenate(key_parts, axis=1)
    value_grad = jnp.concatenate(value_parts, axis=1)
    visual_grad = jnp.dot(key_grad, key_weight.T, preferred_element_type=jnp.float32) + jnp.dot(value_grad, value_weight.T, preferred_element_type=jnp.float32)
    return query_grad, visual_grad.astype(jnp.bfloat16)
```

```python
import functools

import jax
import jax.numpy as jnp
from jax import lax
from jax.experimental import pallas as pl
from jax.experimental.pallas import tpu as pltpu
from jax.sharding import PartitionSpec as P

DH = 128
FRAMES = 8
QBLK = 32
TOK = 128
ROWS = 512
VISUAL = 8192
CHUNKS = 2
PIECE = 256 // CHUNKS
SUB = 512
TILE = 2048
SCALE = DH**-0.5
C2 = SCALE * 1.4426950408889634
BIG = 2.0**100
F32 = jnp.float32
BF16 = jnp.bfloat16
NN = (((1,), (0,)), ((), ()))
NT = (((1,), (1,)), ((), ()))
TN = (((0,), (0,)), ((), ()))


def dot(a, b, dims):
    return lax.dot_general(a, b, dims, preferred_element_type=F32)


def marks(base, rows, first, last):
    at = base + lax.broadcasted_iota(jnp.int32, (rows, 128), 0)
    return jnp.where((at >= first) & (at < last), 1.0, 0.0).astype(BF16)


def pieces(x):
    hi = x.astype(BF16).astype(F32)
    rest = x - hi
    mid = rest.astype(BF16).astype(F32)
    return hi, mid, rest - mid


def stat_rows(top, x):
    hi, mid, low = pieces(x)
    row = lax.broadcasted_iota(jnp.int32, top.shape, 0)
    under = jnp.where(row == 0, hi, jnp.where(row == 1, mid, jnp.where(row == 2, low, 0.0)))
    return jnp.concatenate([top, under], axis=0).astype(BF16)


def stats_kernel(mask_ref, fid_ref, q_ref, d_ref, k_ref, v_ref, own_ref, edge_ref, qt, dt, top, m_ref, l_ref, o_ref):
    step = pl.program_id(0)

    @pl.when(step == 0)
    def _():
        fid = fid_ref[...]
        lane = lax.broadcasted_iota(jnp.int32, (8, 128), 1)
        first = jnp.zeros((8, 128), jnp.int32)
        last = jnp.where(lane < 8 + 3, VISUAL, 0)
        for f in range(1, FRAMES):
            below = jnp.sum((fid < f).astype(F32), axis=(0, 1), keepdims=True).astype(jnp.int32)
            first = jnp.where(lane == f, below, first)
            last = jnp.where(lane == f - 1, below, last)
        edge_ref[0] = first
        edge_ref[1] = last
        sub = lax.broadcasted_iota(jnp.int32, (8, 128), 0)
        bias = jnp.zeros((8, 128), F32)
        for b in range(TOK // QBLK):
            for f in range(FRAMES):
                here = (sub == f) & (lane // QBLK == b)
                bias = jnp.where(here, jnp.where(mask_ref[b, f] == 1, 0.0, -BIG), bias)
        top[...] = jnp.concatenate([bias] * 4, axis=1)
        for h in range(4):
            cols = slice(h * DH, (h + 1) * DH)
            qt[:DH, cols] = q_ref[:, cols].T
            dt[:, cols] = d_ref[:, cols].T
        qt[DH:DH + 16, :] = jnp.concatenate([top[...], jnp.zeros((8, ROWS), F32)], axis=0).astype(BF16)
        qt[DH + 16:, :] = jnp.zeros((DH - 16, ROWS), BF16)
        m_ref[...] = jnp.full((1, ROWS), -3e38, F32)
        l_ref[...] = jnp.zeros((1, ROWS), F32)
        o_ref[...] = jnp.zeros((DH, ROWS), F32)

    first, last = edge_ref[0, 0:1], edge_ref[1, 0:1]
    qa = qt[...]
    m, l, o = m_ref[...], l_ref[...], o_ref[...]
    for s in range(TILE // SUB):
        at = slice(s * SUB, (s + 1) * SUB)
        ka = jnp.concatenate([k_ref[at], marks(step * TILE + s * SUB, SUB, first, last)], axis=1)
        x = dot(ka, qa, NN) * C2
        m_new = jnp.maximum(m, jnp.max(x, axis=0, keepdims=True))
        shrink = jnp.exp2(m - m_new)
        p = jnp.exp2(x - m_new)
        l = l * shrink + jnp.sum(p, axis=0, keepdims=True)
        o = o * shrink + dot(v_ref[at], p.astype(BF16), TN)
        m = m_new
    m_ref[...], l_ref[...], o_ref[...] = m, l, o

    @pl.when(step == VISUAL // TILE - 1)
    def _():
        own_ref[0, :DH] = qt[:DH, :]
        own_ref[0, DH:] = stat_rows(top[...], (m + jnp.log2(l)) * (-1.0 / C2))
        delta = jnp.sum(dt[...].astype(F32) * o, axis=0, keepdims=True) / l
        own_ref[1, :DH] = dt[...]
        own_ref[1, DH:] = stat_rows(jnp.zeros((8, ROWS), F32), -delta)


def softmax_stats(queries, out_grad, keys, values, frame_ids, text_mask):
    whole = lambda *shape: pl.BlockSpec(shape, lambda i: (0,) * len(shape))
    tile = pl.BlockSpec((TILE, DH), lambda i: (i, 0))
    return pl.pallas_call(
        stats_kernel,
        grid=(VISUAL // TILE,),
        in_specs=[
            pl.BlockSpec(memory_space=pltpu.SMEM),
            whole(VISUAL // 128, 128),
            whole(TOK, ROWS),
            whole(TOK, ROWS),
            tile,
            tile,
        ],
        out_specs=[whole(2, DH + 16, ROWS), whole(2, 8, 128)],
        out_shape=[
            jax.ShapeDtypeStruct((2, DH + 16, ROWS), BF16),
            jax.ShapeDtypeStruct((2, 8, 128), jnp.int32),
        ],
        scratch_shapes=[
            pltpu.VMEM((2 * DH, ROWS), BF16),
            pltpu.VMEM((DH, ROWS), BF16),
            pltpu.VMEM((8, ROWS), F32),
            pltpu.VMEM((1, ROWS), F32),
            pltpu.VMEM((1, ROWS), F32),
            pltpu.VMEM((DH, ROWS), F32),
        ],
        compiler_params=pltpu.CompilerParams(vmem_limit_bytes=40 << 20),
        name="softmax_stats",
    )(text_mask, frame_ids.reshape(VISUAL // 128, 128), queries, out_grad, keys, values)


def grads_kernel(chunk, place, k_ref, v_ref, q_ref, d_ref, q2_ref, d2_ref, own_ref, other_ref, edge_ref, *rest):
    if chunk:
        sofar_ref, *rest = rest
    kk, ks, vk, vs, qsum, qt, dt, qr, dr = rest
    y, z, af = place[0], place[1], place[2]
    for side, (b, qq, dd) in enumerate(((own_ref, q_ref, d_ref), (other_ref, q2_ref, d2_ref))):
        cols = slice(side * ROWS, (side + 1) * ROWS)
        qt[:DH + 16, cols] = b[0]
        dt[:DH + 16, cols] = b[1]
        for h in range(4):
            at = slice(side * ROWS + h * TOK, side * ROWS + (h + 1) * TOK)
            qr[at] = qq[:, h * DH:(h + 1) * DH]
            dr[at] = dd[:, h * DH:(h + 1) * DH]
    qt[DH + 16:] = jnp.zeros((DH - 16, 2 * ROWS), BF16)
    dt[DH + 16:] = jnp.zeros((DH - 16, 2 * ROWS), BF16)
    first, last = edge_ref[0, 0:1], edge_ref[1, 0:1]
    total = sofar_ref[...] if chunk else jnp.zeros((DH, 2 * ROWS), F32)
    for r in range(4):
        kl, vl, ml = [], [], []
        for s in range(4):
            kl.append(k_ref[y ^ r, z ^ s, 0, 0])
            vl.append(v_ref[y ^ r, z ^ s, 0, 0])
            ml.append(marks((y ^ r) * 2048 + (z ^ s) * 512 + af * 256 + chunk * PIECE, PIECE, first, last))
        k = jnp.concatenate(kl, axis=0)
        mark = jnp.concatenate(ml, axis=0)
        p = jnp.exp2(dot(jnp.concatenate([k, mark], axis=1), qt[...], NN) * C2)
        dp = dot(jnp.concatenate([jnp.concatenate(vl, axis=0), mark], axis=1), dt[...], NN)
        ds = (p * dp).astype(BF16)
        kp = (dot(ds, qr[...], NN) * SCALE).astype(BF16)
        vp = dot(p.astype(BF16), dr[...], NN).astype(BF16)
        total = total + dot(k, ds, TN)
        kref, kat = ((kk, 0), (ks, 0), (ks, 1), (kk, 1))[r]
        vref, vat = ((vk, 0), (vk, 1), (vs, 1), (vs, 0))[r]
        kref[kat] = kp
        vref[vat] = vp
    qsum[...] = total


def chunk_grads(chunk, place, keys, values, q, d, q2, d2, own, other, edge, sofar):
    view = (4, 4, 2, CHUNKS, PIECE, DH)
    block = pl.BlockSpec((4, 4, 1, 1, PIECE, DH), lambda i, p: (0, 0, p[2], chunk, 0, 0))
    whole = lambda *shape: pl.BlockSpec(shape, lambda i, p: (0,) * len(shape))
    part = jax.ShapeDtypeStruct((2, 4 * PIECE, DH), BF16)
    more = [] if sofar is None else [sofar]
    return pl.pallas_call(
        functools.partial(grads_kernel, chunk),
        grid_spec=pltpu.PrefetchScalarGridSpec(
            num_scalar_prefetch=1,
            grid=(1,),
            in_specs=[block, block]
            + [whole(TOK, ROWS)] * 4
            + [whole(2, DH + 16, ROWS)] * 2
            + [whole(2, 8, 128)]
            + [whole(DH, 2 * ROWS)] * len(more),
            out_specs=[whole(2, 4 * PIECE, DH)] * 4 + [whole(DH, 2 * ROWS)],
            scratch_shapes=[
                pltpu.VMEM((2 * DH, 2 * ROWS), BF16),
                pltpu.VMEM((2 * DH, 2 * ROWS), BF16),
                pltpu.VMEM((2 * ROWS, DH), BF16),
                pltpu.VMEM((2 * ROWS, DH), BF16),
            ],
        ),
        out_shape=[part] * 4 + [jax.ShapeDtypeStruct((DH, 2 * ROWS), F32)],
        compiler_params=pltpu.CompilerParams(vmem_limit_bytes=48 << 20),
        name=f"chunk_grads_{chunk}",
    )(place, keys.reshape(view), values.reshape(view), q, d, q2, d2, own, other, edge, *more)


def query_kernel(mine_ref, got_ref, out_ref):
    total = (mine_ref[...] + got_ref[...].astype(F32)) * SCALE
    for h in range(4):
        out_ref[:, h * DH:(h + 1) * DH] = total[:, h * TOK:(h + 1) * TOK].T.astype(BF16)


def query_out(sums, got):
    return pl.pallas_call(
        query_kernel,
        grid=(1,),
        in_specs=[pl.BlockSpec((DH, ROWS), lambda i: (0, 0))] * 2,
        out_specs=pl.BlockSpec((TOK, ROWS), lambda i: (0, 0)),
        out_shape=jax.ShapeDtypeStruct((TOK, ROWS), BF16),
        name="query_out",
    )(sums, got)


def visual_kernel(place, mine_ref, other_ref, *rest):
    *parts, out_ref = rest
    af, x, zl = place[2], place[3], place[4]
    for ref, half in ((mine_ref, af), (other_ref, 1 - af)):
        total = jnp.zeros((256, 512), F32)
        for k in range(4):
            for e in range(2):
                source = ((x - k) & 3) * 2 + (zl ^ e)
                g = jnp.concatenate([parts[c * 4 + k][e] for c in range(CHUNKS)], axis=0)
                total = total + dot(g, ref[source], NT)
        out_ref[:, pl.ds(pl.multiple_of(half * 512, 512), 512)] = total.astype(BF16)


def visual_out(place, mine, other, parts):
    whole = lambda *shape: pl.BlockSpec(shape, lambda i, p: (0,) * len(shape))
    return pl.pallas_call(
        visual_kernel,
        grid_spec=pltpu.PrefetchScalarGridSpec(
            num_scalar_prefetch=1,
            grid=(1,),
            in_specs=[whole(8, 512, 256)] * 2 + [whole(2, PIECE, 256)] * len(parts),
            out_specs=whole(256, 1024),
        ),
        out_shape=jax.ShapeDtypeStruct((256, 1024), BF16),
        compiler_params=pltpu.CompilerParams(vmem_limit_bytes=32 << 20),
        name="visual_out",
    )(place, mine, other, *parts)


def swap_cores(a):
    return lax.ppermute(a, "af", [(0, 1), (1, 0)])


def along_y(a, bit):
    return lax.ppermute(a, "pb", [(i, i ^ (4 * bit)) for i in range(16)])


def along_z(a, bit):
    return lax.ppermute(a, "pb", [(i, i ^ bit) for i in range(16)])


def along_x(a, k):
    return lax.ppermute(a, "ha", [(i, (i + 2 * k) % 8) for i in range(8)])


def add(a, b):
    return (a.astype(F32) + b.astype(F32)).astype(BF16)


def reduce_chunk(kk, ks, vk, vs):
    rk, rv = along_y(ks, 1), along_y(vs, 3)
    rk2 = along_y(add(kk[1], rk[1]), 3)
    rv2 = along_y(add(vk[1], rv[1]), 1)
    k = (kk[0].astype(F32) + rk[0].astype(F32) + rk2.astype(F32)).astype(BF16).reshape(4, PIECE, DH)
    v = (vk[0].astype(F32) + rv[0].astype(F32) + rv2.astype(F32)).astype(BF16).reshape(4, PIECE, DH)
    rk, rv = along_z(k[1:3], 1), along_z(v[2:4], 3)
    rk2 = along_z(add(k[3], rk[1]), 3)
    rv2 = along_z(add(v[1], rv[0]), 1)
    k = (k[0].astype(F32) + rk[0].astype(F32) + rk2.astype(F32)).astype(BF16)
    v = (v[0].astype(F32) + rv[1].astype(F32) + rv2.astype(F32)).astype(BF16)
    g = jnp.concatenate([k, v], axis=1)
    pair = jnp.stack([g, lax.ppermute(g, "ha", [(i, i ^ 1) for i in range(8)])])
    return [pair] + [along_x(pair, i) for i in (1, 2, 3)]


def on_device(queries, vis_keys, vis_values, out_grad, key_weight, value_weight, frame_ids, text_mask):
    pb, ha, af = lax.axis_index("pb"), lax.axis_index("ha"), lax.axis_index("af")
    place = jnp.stack([pb // 4, pb % 4, af, ha // 2, ha % 2]).astype(jnp.int32)
    queries2, out_grad2 = swap_cores(queries), swap_cores(out_grad)
    half = lambda w: lax.dynamic_index_in_dim(w.reshape(8, 2, 512, DH), af, 1, keepdims=False)
    weights = jnp.concatenate([half(key_weight), half(value_weight)], axis=2)
    weights = lax.all_to_all(weights, "ha", 0, 0, tiled=True)
    weights2 = swap_cores(weights)
    own, edge = softmax_stats(queries, out_grad, vis_keys, vis_values, frame_ids, text_mask)
    other = swap_cores(own)
    qsum, parts = None, []
    for chunk in range(CHUNKS):
        kk, ks, vk, vs, qsum = chunk_grads(
            chunk, place, vis_keys, vis_values, queries, out_grad, queries2, out_grad2, own, other, edge, qsum
        )
        parts += reduce_chunk(kk, ks, vk, vs)
    query_grad = query_out(qsum[:, :ROWS], swap_cores(qsum[:, ROWS:].astype(BF16)))
    visual_grad = visual_out(place, weights, weights2, parts)
    return query_grad, visual_grad


def solution(mesh):
    in_specs = (
        P("pb", ("ha", "af")),
        P(None, "ha"),
        P(None, "ha"),
        P("pb", ("ha", "af")),
        P(None, "ha"),
        P(None, "ha"),
        P(),
        P("pb", None),
    )
    out_specs = (P("pb", ("ha", "af")), P(("pb", "af"), "ha"))
    return jax.shard_map(on_device, mesh=mesh, in_specs=in_specs, out_specs=out_specs, check_vma=False)
```

```python
import functools

import jax
import jax.numpy as jnp
from jax import lax
from jax.experimental import pallas as pl
from jax.experimental.pallas import tpu as pltpu
from jax.sharding import PartitionSpec as P

DH = 128
FRAMES = 8
QBLK = 32
TOK = 128
ROWS = 512
VISUAL = 8192
CHUNKS = 2
PIECE = 256 // CHUNKS
SUB = 512
TILE = 2048
SCALE = DH**-0.5
C2 = SCALE * 1.4426950408889634
BIG = 2.0**100
VMEM_A = 60
VMEM_B = 58
F32 = jnp.float32
BF16 = jnp.bfloat16
NN = (((1,), (0,)), ((), ()))
NT = (((1,), (1,)), ((), ()))
TN = (((0,), (0,)), ((), ()))


def dot(a, b, dims):
    return lax.dot_general(a, b, dims, preferred_element_type=F32)


def cost(us):
    return pl.CostEstimate(flops=int(us * 1.1e9), transcendentals=0, bytes_accessed=1 << 20)


def marks(base, rows, first, last):
    at = base + lax.broadcasted_iota(jnp.int32, (rows, 128), 0)
    return jnp.where((at >= first) & (at < last), 1.0, 0.0).astype(BF16)


def pieces(x):
    hi = x.astype(BF16).astype(F32)
    rest = x - hi
    mid = rest.astype(BF16).astype(F32)
    return hi, mid, rest - mid


def stat_rows(top, x):
    hi, mid, low = pieces(x)
    row = lax.broadcasted_iota(jnp.int32, top.shape, 0)
    under = jnp.where(row == 0, hi, jnp.where(row == 1, mid, jnp.where(row == 2, low, 0.0)))
    return jnp.concatenate([top, under], axis=0).astype(BF16)


def stats_kernel(
    mask_ref, fid_ref, q_ref, d_ref, k_hbm, v_hbm, kw_hbm, vw_hbm, own_ref, edge_ref, w_hbm, k_ref, v_ref, qt, dt, sems, wsem
):
    af = lax.axis_index("af")
    loads = []
    for t in range(VISUAL // TILE):
        at = pl.ds(t * TILE, TILE)
        loads.append(
            [
                pltpu.make_async_copy(k_hbm.at[at], k_ref.at[at], sems.at[0, t]),
                pltpu.make_async_copy(v_hbm.at[at], v_ref.at[at], sems.at[1, t]),
            ]
        )
        for load in loads[t]:
            load.start()
    moves = [pltpu.make_async_copy(w.at[:, af], w_hbm.at[:, i], wsem.at[i]) for i, w in enumerate((kw_hbm, vw_hbm))]
    for move in moves:
        move.start()
    fid = fid_ref[...]
    lane = lax.broadcasted_iota(jnp.int32, (8, 128), 1)
    first = jnp.zeros((8, 128), jnp.int32)
    last = jnp.where(lane < 8 + 3, VISUAL, 0)
    for f in range(1, FRAMES):
        below = jnp.sum((fid < f).astype(F32), axis=(0, 1), keepdims=True).astype(jnp.int32)
        first = jnp.where(lane == f, below, first)
        last = jnp.where(lane == f - 1, below, last)
    edge_ref[0] = first
    edge_ref[1] = last
    first, last = first[0:1], last[0:1]
    sub = lax.broadcasted_iota(jnp.int32, (8, 128), 0)
    bias = jnp.zeros((8, 128), F32)
    for b in range(TOK // QBLK):
        for f in range(FRAMES):
            here = (sub == f) & (lane // QBLK == b)
            bias = jnp.where(here, jnp.where(mask_ref[b, f] == 1, 0.0, -BIG), bias)
    top = jnp.concatenate([bias] * 4, axis=1)
    for h in range(4):
        cols = slice(h * DH, (h + 1) * DH)
        qt[:DH, cols] = q_ref[:, cols].T
        dt[:, cols] = d_ref[:, cols].T
    qt[DH:DH + 16, :] = jnp.concatenate([top, jnp.zeros((8, ROWS), F32)], axis=0).astype(BF16)
    qt[DH + 16:, :] = jnp.zeros((DH - 16, ROWS), BF16)
    own_ref[0, :DH] = qt[:DH, :]
    own_ref[1, :DH] = dt[...]
    own_ref[0, DH + 16:] = q_ref[...]
    own_ref[1, DH + 16:] = d_ref[...]
    m = jnp.full((1, ROWS), -3e38, F32)
    l = jnp.zeros((1, ROWS), F32)
    o = jnp.zeros((DH, ROWS), F32)
    for s in range(VISUAL // SUB):
        if s % (TILE // SUB) == 0:
            for load in loads[s // (TILE // SUB)]:
                load.wait()
        at = slice(s * SUB, (s + 1) * SUB)
        ka = jnp.concatenate([k_ref[at], marks(s * SUB, SUB, first, last)], axis=1)
        x = dot(ka, qt[...], NN) * C2
        m_new = jnp.maximum(m, jnp.max(x, axis=0, keepdims=True))
        shrink = jnp.exp2(m - m_new)
        p = jnp.exp2(x - m_new)
        l = l * shrink + jnp.sum(p, axis=0, keepdims=True)
        o = o * shrink + dot(v_ref[at], p.astype(BF16), TN)
        m = m_new
    own_ref[0, DH:DH + 16] = stat_rows(top, (m + jnp.log2(l)) * (-1.0 / C2))
    delta = jnp.sum(dt[...].astype(F32) * o, axis=0, keepdims=True) / l
    own_ref[1, DH:DH + 16] = stat_rows(jnp.zeros((8, ROWS), F32), -delta)
    for move in moves:
        move.wait()


def softmax_stats(queries, out_grad, keys, values, frame_ids, text_mask, key_weight, value_weight):
    vmem, far = pl.BlockSpec(memory_space=pltpu.VMEM), pl.BlockSpec(memory_space=pltpu.HBM)
    return pl.pallas_call(
        stats_kernel,
        in_specs=[pl.BlockSpec(memory_space=pltpu.SMEM), vmem, vmem, vmem, far, far, far, far],
        out_specs=[vmem, vmem, far],
        out_shape=[
            jax.ShapeDtypeStruct((2, DH + 16 + TOK, ROWS), BF16),
            jax.ShapeDtypeStruct((2, 8, 128), jnp.int32),
            jax.ShapeDtypeStruct((8, 2, 512, DH), BF16),
        ],
        scratch_shapes=[
            pltpu.VMEM((VISUAL, DH), BF16),
            pltpu.VMEM((VISUAL, DH), BF16),
            pltpu.VMEM((2 * DH, ROWS), BF16),
            pltpu.VMEM((DH, ROWS), BF16),
            pltpu.SemaphoreType.DMA((2, VISUAL // TILE)),
            pltpu.SemaphoreType.DMA((2,)),
        ],
        compiler_params=pltpu.CompilerParams(vmem_limit_bytes=VMEM_A << 20),
        cost_estimate=cost(10),
        name="softmax_stats",
    )(
        text_mask,
        frame_ids.reshape(VISUAL // 128, 128),
        queries,
        out_grad,
        keys,
        values,
        key_weight.reshape(8, 2, 512, DH),
        value_weight.reshape(8, 2, 512, DH),
    )


def grads_kernel(chunk, place, k_hbm, v_hbm, own_ref, other_ref, edge_ref, *rest):
    if chunk:
        sofar_ref, *rest = rest
    if chunk == CHUNKS - 1:
        keep_ref, send_ref, qown_ref, qother_ref, *rest = rest
    else:
        keep_ref, send_ref, qsum_ref, *rest = rest
    qt, dt, qr, dr, k_ref, v_ref, sems = rest
    y, z, af = place[0], place[1], place[2]
    order = (0, 3 - 2 * af, 1 + 2 * af, 2)
    loads = []
    for r in range(4):
        loads.append(
            [
                pltpu.make_async_copy(hbm.at[y ^ order[r], :, af, chunk], ref.at[r], sems.at[i, r])
                for i, (hbm, ref) in enumerate(((k_hbm, k_ref), (v_hbm, v_ref)))
            ]
        )
        for load in loads[r]:
            load.start()
    for side, ref in enumerate((own_ref, other_ref)):
        cols = slice(side * ROWS, (side + 1) * ROWS)
        qt[:DH + 16, cols] = ref[0, :DH + 16]
        dt[:DH + 16, cols] = ref[1, :DH + 16]
        for h in range(4):
            at = slice(side * ROWS + h * TOK, side * ROWS + (h + 1) * TOK)
            qr[at] = ref[0, DH + 16:, h * DH:(h + 1) * DH]
            dr[at] = ref[1, DH + 16:, h * DH:(h + 1) * DH]
    qt[DH + 16:] = jnp.zeros((DH - 16, 2 * ROWS), BF16)
    dt[DH + 16:] = jnp.zeros((DH - 16, 2 * ROWS), BF16)
    first, last = edge_ref[0, 0:1], edge_ref[1, 0:1]
    total = sofar_ref[...] if chunk else jnp.zeros((DH, 2 * ROWS), F32)
    for r in range(4):
        for load in loads[r]:
            load.wait()
        kl, vl, ml = [], [], []
        for s in range(4):
            yy, zz = y ^ order[r], z ^ order[s]
            kl.append(k_ref[r, zz])
            vl.append(v_ref[r, zz])
            ml.append(marks(yy * 2048 + zz * 512 + af * 256 + chunk * PIECE, PIECE, first, last))
        k = jnp.concatenate(kl, axis=0)
        mark = jnp.concatenate(ml, axis=0)
        p = jnp.exp2(dot(jnp.concatenate([k, mark], axis=1), qt[...], NN) * C2)
        dp = dot(jnp.concatenate([jnp.concatenate(vl, axis=0), mark], axis=1), dt[...], NN)
        ds = (p * dp).astype(BF16)
        out = (keep_ref, send_ref)[r // 2]
        out[r % 2, :, :DH] = (dot(ds, qr[...], NN) * SCALE).astype(BF16)
        out[r % 2, :, DH:] = dot(p.astype(BF16), dr[...], NN).astype(BF16)
        total = total + dot(k, ds, TN)
    if chunk == CHUNKS - 1:
        qown_ref[...] = total[:, :ROWS]
        qother_ref[...] = total[:, ROWS:].astype(BF16)
    else:
        qsum_ref[...] = total


def chunk_grads(chunk, place, keys, values, own, other, edge, sofar):
    view = (4, 4, 2, CHUNKS, PIECE, DH)
    vmem, far = pl.BlockSpec(memory_space=pltpu.VMEM), pl.BlockSpec(memory_space=pltpu.HBM)
    part = jax.ShapeDtypeStruct((2, 4 * PIECE, 2 * DH), BF16)
    more = [] if sofar is None else [sofar]
    if chunk == CHUNKS - 1:
        sums = [jax.ShapeDtypeStruct((DH, ROWS), F32), jax.ShapeDtypeStruct((DH, ROWS), BF16)]
    else:
        sums = [jax.ShapeDtypeStruct((DH, 2 * ROWS), F32)]
    outs = [part, part] + sums
    return pl.pallas_call(
        functools.partial(grads_kernel, chunk),
        in_specs=[pl.BlockSpec(memory_space=pltpu.SMEM), far, far] + [vmem] * (3 + len(more)),
        out_specs=[vmem] * len(outs),
        scratch_shapes=[
            pltpu.VMEM((2 * DH, 2 * ROWS), BF16),
            pltpu.VMEM((2 * DH, 2 * ROWS), BF16),
            pltpu.VMEM((2 * ROWS, DH), BF16),
            pltpu.VMEM((2 * ROWS, DH), BF16),
            pltpu.VMEM((4, 4, PIECE, DH), BF16),
            pltpu.VMEM((4, 4, PIECE, DH), BF16),
            pltpu.SemaphoreType.DMA((2, 4)),
        ],
        out_shape=outs,
        compiler_params=pltpu.CompilerParams(vmem_limit_bytes=VMEM_B << 20),
        cost_estimate=cost(14 / CHUNKS),
        name=f"chunk_grads_{chunk}",
    )(place, keys.reshape(view), values.reshape(view), own, other, edge, *more)


def query_kernel(mine_ref, got_ref, out_ref):
    total = (mine_ref[...] + got_ref[...].astype(F32)) * SCALE
    for h in range(4):
        out_ref[:, h * DH:(h + 1) * DH] = total[:, h * TOK:(h + 1) * TOK].T.astype(BF16)


def query_out(sums, got):
    return pl.pallas_call(
        query_kernel,
        in_specs=[pl.BlockSpec(memory_space=pltpu.VMEM)] * 2,
        out_specs=pl.BlockSpec(memory_space=pltpu.VMEM),
        out_shape=jax.ShapeDtypeStruct((TOK, ROWS), BF16),
        cost_estimate=cost(1),
        name="query_out",
    )(sums, got)


def visual_kernel(place, mine_ref, other_ref, *rest):
    *parts, out_ref = rest
    af, ha = place[2], place[3]
    first = jnp.where(af == 0, 1, 6)
    second = jnp.where(af == 0, 2, 1)
    third = jnp.where(af == 0, 6, 2)
    for ref, half in ((mine_ref, af), (other_ref, 1 - af)):
        total = jnp.zeros((256, 512), F32)
        for k in range(8):
            source = ha
            for bit, mask in ((1, first), (2, second), (4, third)):
                if k & bit:
                    source = source ^ mask
            g = jnp.concatenate([parts[c * 2 + k // 4][k % 4] for c in range(CHUNKS)], axis=0)
            w = jnp.concatenate([ref[source, 0], ref[source, 1]], axis=1)
            total = total + dot(g, w, NT)
        out_ref[:, pl.ds(pl.multiple_of(half * 512, 512), 512)] = total.astype(BF16)


def visual_out(place, mine, other, parts):
    vmem = pl.BlockSpec(memory_space=pltpu.VMEM)
    return pl.pallas_call(
        visual_kernel,
        in_specs=[pl.BlockSpec(memory_space=pltpu.SMEM)] + [vmem] * (2 + len(parts)),
        out_specs=vmem,
        out_shape=jax.ShapeDtypeStruct((256, 1024), BF16),
        compiler_params=pltpu.CompilerParams(vmem_limit_bytes=24 << 20),
        cost_estimate=cost(3),
        name="visual_out",
    )(place, mine, other, *parts)


def swap_cores(a):
    return lax.ppermute(a, "af", [(0, 1), (1, 0)])


def pair(a, axis, masks):
    count = {"pb": 16, "ha": 8}[axis]
    return lax.ppermute(a, (axis, "af"), [(2 * i + c, 2 * (i ^ masks[c]) + c) for i in range(count) for c in range(2)])


def plus(*terms):
    return functools.reduce(jnp.add, [t.astype(F32) for t in terms]).astype(BF16)


def reduce_chunk(keep, got):
    got2 = pair(plus(keep[1], got[1]), "pb", (12, 4))
    part = plus(keep[0], got[0], got2).reshape(4, PIECE, 2 * DH)
    got = pair(part[2:], "pb", (1, 3))
    got2 = pair(plus(part[1], got[1]), "pb", (3, 1))
    return plus(part[0], got[0], got2)[None]


def gather_chunk(g):
    g = jnp.concatenate([g, pair(g, "ha", (1, 6))], axis=0)
    g = jnp.concatenate([g, pair(g, "ha", (2, 1))], axis=0)
    return [g, pair(g, "ha", (6, 2))]


def on_device(queries, vis_keys, vis_values, out_grad, key_weight, value_weight, frame_ids, text_mask):
    pb, ha, af = lax.axis_index("pb"), lax.axis_index("ha"), lax.axis_index("af")
    place = jnp.stack([pb // 4, pb % 4, af, ha]).astype(jnp.int32)
    own, edge, weights = softmax_stats(
        queries, out_grad, vis_keys, vis_values, frame_ids, text_mask, key_weight, value_weight
    )
    other = swap_cores(own)
    qsum, parts = None, []
    kept, sent = [], []
    for chunk in range(CHUNKS):
        keep, send, *qsum = chunk_grads(
            chunk, place, vis_keys, vis_values, own, other, edge, qsum[0] if chunk else None
        )
        if chunk == 0:
            weights, keep = lax.optimization_barrier((weights, keep))
            weights = lax.all_to_all(weights, "ha", 0, 0, tiled=True)
            weights2 = swap_cores(weights)
        else:
            send, sent[-1] = lax.optimization_barrier((send, sent[-1]))
        kept.append(keep)
        sent.append(pair(send, "pb", (4, 12)))
    for chunk in range(CHUNKS):
        g = reduce_chunk(kept[chunk], sent[chunk])
        if chunk == CHUNKS - 1:
            query_grad = query_out(qsum[0], swap_cores(qsum[1]))
            g, query_grad = lax.optimization_barrier((g, query_grad))
        parts += gather_chunk(g)
    visual_grad = visual_out(place, weights, weights2, parts)
    return query_grad, visual_grad


def solution(mesh):
    in_specs = (
        P("pb", ("ha", "af")),
        P(None, "ha"),
        P(None, "ha"),
        P("pb", ("ha", "af")),
        P(None, "ha"),
        P(None, "ha"),
        P(),
        P("pb", None),
    )
    out_specs = (P("pb", ("ha", "af")), P(("pb", "af"), "ha"))
    return jax.shard_map(on_device, mesh=mesh, in_specs=in_specs, out_specs=out_specs, check_vma=False)
```

```python
import functools

import jax
import jax.numpy as jnp
from jax import lax
from jax.experimental import pallas as pl
from jax.experimental.pallas import tpu as pltpu
from jax.sharding import PartitionSpec as P

DH = 128
FRAMES = 8
QBLK = 32
TOK = 128
ROWS = 512
VISUAL = 8192
PIECE = 256
SUB = 512
HALF = VISUAL // 2
TILE = 1024
SCALE = DH**-0.5
C2 = SCALE * 1.4426950408889634
BIG = 2.0**100
VMEM_A = 60
VMEM_B = 58
F32 = jnp.float32
BF16 = jnp.bfloat16
NN = (((1,), (0,)), ((), ()))
NT = (((1,), (1,)), ((), ()))
TN = (((0,), (0,)), ((), ()))


def dot(a, b, dims):
    return lax.dot_general(a, b, dims, preferred_element_type=F32)


def cost(us):
    return pl.CostEstimate(flops=int(us * 1.1e9), transcendentals=0, bytes_accessed=1 << 20)


def marks(base, rows, first, last):
    at = base + lax.broadcasted_iota(jnp.int32, (rows, 128), 0)
    return jnp.where((at >= first) & (at < last), 1.0, 0.0).astype(BF16)


def pieces(x):
    hi = x.astype(BF16).astype(F32)
    rest = x - hi
    mid = rest.astype(BF16).astype(F32)
    return hi, mid, rest - mid


def stat_rows(top, x):
    hi, mid, low = pieces(x)
    row = lax.broadcasted_iota(jnp.int32, top.shape, 0)
    under = jnp.where(row == 0, hi, jnp.where(row == 1, mid, jnp.where(row == 2, low, 0.0)))
    return jnp.concatenate([top, under], axis=0).astype(BF16)


def stats_kernel(half, *refs):
    refs = list(refs)
    take = lambda n: [refs.pop(0) for _ in range(n)]
    if half == 0:
        mask_ref, fid_ref, qd_ref, k_hbm, v_hbm, kw_hbm, vw_hbm = take(7)
        qt, dt, state, edge_ref, w_hbm = take(5)
        k_ref, v_ref, sems, w_ref, wsem = refs
    else:
        k_hbm, v_hbm, qt, dt, state, edge_ref, stat_ref, k_ref, v_ref, sems = refs
    loads = []
    for t in range(HALF // TILE):
        at, far = pl.ds(t * TILE, TILE), pl.ds(half * HALF + t * TILE, TILE)
        loads.append(
            [
                pltpu.make_async_copy(k_hbm.at[far], k_ref.at[at], sems.at[0, t]),
                pltpu.make_async_copy(v_hbm.at[far], v_ref.at[at], sems.at[1, t]),
            ]
        )
        for load in loads[t]:
            load.start()
    if half == 0:
        af = lax.axis_index("af")
        moves = [pltpu.make_async_copy(w.at[:, af], w_ref.at[i], wsem.at[i]) for i, w in enumerate((kw_hbm, vw_hbm))]
        backs = [pltpu.make_async_copy(w_ref.at[i], w_hbm.at[:, i], wsem.at[2 + i]) for i in range(2)]
        for move in moves:
            move.start()
        fid = fid_ref[...]
        lane = lax.broadcasted_iota(jnp.int32, (8, 128), 1)
        first = jnp.zeros((8, 128), jnp.int32)
        last = jnp.where(lane < 8 + 3, VISUAL, 0)
        for f in range(1, FRAMES):
            below = jnp.sum((fid < f).astype(F32), axis=(0, 1), keepdims=True).astype(jnp.int32)
            first = jnp.where(lane == f, below, first)
            last = jnp.where(lane == f - 1, below, last)
        edge_ref[0] = first
        edge_ref[1] = last
        sub = lax.broadcasted_iota(jnp.int32, (8, 128), 0)
        bias = jnp.zeros((8, 128), F32)
        for b in range(TOK // QBLK):
            for f in range(FRAMES):
                here = (sub == f) & (lane // QBLK == b)
                bias = jnp.where(here, jnp.where(mask_ref[b, f] == 1, 0.0, -BIG), bias)
        top = jnp.concatenate([bias] * 4, axis=1)
        for h in range(4):
            cols = slice(h * DH, (h + 1) * DH)
            qt[:DH, cols] = qd_ref[0, :, cols].T
            dt[:, cols] = qd_ref[1, :, cols].T
        qt[DH:DH + 16, :] = jnp.concatenate([top, jnp.zeros((8, ROWS), F32)], axis=0).astype(BF16)
        qt[DH + 16:, :] = jnp.zeros((DH - 16, ROWS), BF16)
        m = jnp.full((1, ROWS), -3e38, F32)
        l = jnp.zeros((1, ROWS), F32)
        o = jnp.zeros((DH, ROWS), F32)
    else:
        m, l, o = state[DH:DH + 1], state[DH + 8:DH + 9], state[:DH]
    first, last = edge_ref[0, 0:1], edge_ref[1, 0:1]
    for s in range(HALF // SUB):
        if s % (TILE // SUB) == 0:
            for load in loads[s // (TILE // SUB)]:
                load.wait()
        if half == 0 and s == HALF // SUB // 2:
            for move, back in zip(moves, backs):
                move.wait()
                back.start()
        at = slice(s * SUB, (s + 1) * SUB)
        ka = jnp.concatenate([k_ref[at], marks(half * HALF + s * SUB, SUB, first, last)], axis=1)
        x = dot(ka, qt[...], NN) * C2
        m_new = jnp.maximum(m, jnp.max(x, axis=0, keepdims=True))
        shrink = jnp.exp2(m - m_new)
        p = jnp.exp2(x - m_new)
        l = l * shrink + jnp.sum(p, axis=0, keepdims=True)
        o = o * shrink + dot(v_ref[at], p.astype(BF16), TN)
        m = m_new
    if half == 0:
        state[:DH] = o
        state[DH:DH + 8] = jnp.broadcast_to(m, (8, ROWS))
        state[DH + 8:] = jnp.broadcast_to(l, (8, ROWS))
        for back in backs:
            back.wait()
    else:
        delta = jnp.sum(dt[...].astype(F32) * o, axis=0, keepdims=True) / l
        stat_ref[0] = stat_rows(qt[DH:DH + 8].astype(F32), (m + jnp.log2(l)) * (-1.0 / C2))
        stat_ref[1] = stat_rows(jnp.zeros((8, ROWS), F32), -delta)


def softmax_stats(half, *args):
    vmem, far = pl.BlockSpec(memory_space=pltpu.VMEM), pl.BlockSpec(memory_space=pltpu.HBM)
    scratch = [
        pltpu.VMEM((HALF, DH), BF16),
        pltpu.VMEM((HALF, DH), BF16),
        pltpu.SemaphoreType.DMA((2, HALF // TILE)),
    ]
    if half == 0:
        in_specs = [pl.BlockSpec(memory_space=pltpu.SMEM), vmem, vmem, far, far, far, far]
        out_specs = [vmem] * 4 + [far]
        outs = [
            jax.ShapeDtypeStruct((2 * DH, ROWS), BF16),
            jax.ShapeDtypeStruct((DH, ROWS), BF16),
            jax.ShapeDtypeStruct((DH + 16, ROWS), F32),
            jax.ShapeDtypeStruct((2, 8, 128), jnp.int32),
            jax.ShapeDtypeStruct((8, 2, 512, DH), BF16),
        ]
        scratch += [pltpu.VMEM((2, 8, 512, DH), BF16), pltpu.SemaphoreType.DMA((4,))]
    else:
        in_specs = [far, far] + [vmem] * 4
        out_specs = vmem
        outs = jax.ShapeDtypeStruct((2, 16, ROWS), BF16)
    return pl.pallas_call(
        functools.partial(stats_kernel, half),
        in_specs=in_specs,
        out_specs=out_specs,
        out_shape=outs,
        scratch_shapes=scratch,
        compiler_params=pltpu.CompilerParams(vmem_limit_bytes=VMEM_A << 20),
        cost_estimate=cost(6),
        name=f"softmax_stats_{half}",
    )(*args)


def grads_kernel(place, k_hbm, v_hbm, edge_ref, own_ref, other_ref, ostat_ref, pstat_ref, part_ref, qsum_ref, *scratch):
    ka, va, kt, ksum, vsum, k_ref, v_ref, sems = scratch
    y, z, af = place[0], place[1], place[2]
    order = (0, 3 - 2 * af, 1 + 2 * af, 2)
    loads = []
    for i, (hbm, ref) in enumerate(((k_hbm, k_ref), (v_hbm, v_ref))):
        loads.append(pltpu.make_async_copy(hbm.at[y, :, af], ref, sems.at[i]))
        loads[i].start()
    first, last = edge_ref[0, 0:1], edge_ref[1, 0:1]
    for s in range(4):
        at = slice(s * PIECE, (s + 1) * PIECE)
        mark = marks(y * 2048 + (z ^ order[s]) * 512 + af * 256, PIECE, first, last)
        ka[at, DH:] = mark
        va[at, DH:] = mark
    for load in loads:
        load.wait()
    for s in range(4):
        at = slice(s * PIECE, (s + 1) * PIECE)
        k = k_ref[z ^ order[s]]
        ka[at, :DH] = k
        va[at, :DH] = v_ref[z ^ order[s]]
        kt[:, at] = k.T
    for block in range(8):
        side, slot = block // 4, block % 4
        raw, stat = ((own_ref, ostat_ref), (other_ref, pstat_ref))[side]
        heads = [slice(h * DH, (h + 1) * DH) for h in range(4)]
        empty = jnp.zeros((DH - 16, ROWS), BF16)
        qt = jnp.concatenate(
            [jnp.concatenate([raw[slot, 0, :, h].T for h in heads], axis=1), stat[slot, 0], empty], axis=0
        )
        dt = jnp.concatenate(
            [jnp.concatenate([raw[slot, 1, :, h].T for h in heads], axis=1), stat[slot, 1], empty], axis=0
        )
        qr = jnp.concatenate([raw[slot, 0, :, h] for h in heads], axis=0)
        dr = jnp.concatenate([raw[slot, 1, :, h] for h in heads], axis=0)
        total = jnp.zeros((DH, ROWS), F32)
        for t in range(2):
            at = slice(t * 512, (t + 1) * 512)
            p = jnp.exp2(dot(ka[at], qt, NN) * C2)
            ds = (p * dot(va[at], dt, NN)).astype(BF16)
            kp = dot(ds, qr, NN)
            vp = dot(p.astype(BF16), dr, NN)
            if block:
                kp = kp + ksum[at]
                vp = vp + vsum[at]
            if block < 7:
                ksum[at] = kp
                vsum[at] = vp
            else:
                for s in range(2):
                    rows = slice(s * PIECE, (s + 1) * PIECE)
                    part_ref[2 * t + s, :, :DH] = (kp[rows] * SCALE).astype(BF16)
                    part_ref[2 * t + s, :, DH:] = vp[rows].astype(BF16)
            total = total + dot(kt[:, at], ds, NN)
        qsum_ref[side, slot] = total.astype(BF16)


def visual_token_grads(place, keys, values, edge, *rest):
    view = (4, 4, 2, PIECE, DH)
    vmem, far = pl.BlockSpec(memory_space=pltpu.VMEM), pl.BlockSpec(memory_space=pltpu.HBM)
    return pl.pallas_call(
        grads_kernel,
        in_specs=[pl.BlockSpec(memory_space=pltpu.SMEM), far, far] + [vmem] * 5,
        out_specs=[vmem, vmem],
        out_shape=[
            jax.ShapeDtypeStruct((4, PIECE, 2 * DH), BF16),
            jax.ShapeDtypeStruct((2, 4, DH, ROWS), BF16),
        ],
        scratch_shapes=[
            pltpu.VMEM((4 * PIECE, 2 * DH), BF16),
            pltpu.VMEM((4 * PIECE, 2 * DH), BF16),
            pltpu.VMEM((DH, 4 * PIECE), BF16),
            pltpu.VMEM((4 * PIECE, DH), F32),
            pltpu.VMEM((4 * PIECE, DH), F32),
            pltpu.VMEM((4, PIECE, DH), BF16),
            pltpu.VMEM((4, PIECE, DH), BF16),
            pltpu.SemaphoreType.DMA((2,)),
        ],
        compiler_params=pltpu.CompilerParams(vmem_limit_bytes=VMEM_B << 20),
        cost_estimate=cost(14),
        name="visual_token_grads",
    )(place, keys.reshape(view), values.reshape(view), edge, *rest)


def query_kernel(mine_ref, got_ref, out_ref):
    total = (mine_ref[...].astype(F32) + got_ref[...].astype(F32)) * SCALE
    for h in range(4):
        out_ref[:, h * DH:(h + 1) * DH] = total[:, h * TOK:(h + 1) * TOK].T.astype(BF16)


def query_out(mine, got):
    return pl.pallas_call(
        query_kernel,
        in_specs=[pl.BlockSpec(memory_space=pltpu.VMEM)] * 2,
        out_specs=pl.BlockSpec(memory_space=pltpu.VMEM),
        out_shape=jax.ShapeDtypeStruct((TOK, ROWS), BF16),
        cost_estimate=cost(1),
        name="query_out",
    )(mine, got)


def visual_kernel(place, mine_ref, other_ref, near_ref, far_ref, out_ref):
    af, ha = place[2], place[3]
    first = jnp.where(af == 0, 1, 6)
    second = jnp.where(af == 0, 2, 1)
    third = jnp.where(af == 0, 6, 2)
    for ref, half in ((mine_ref, af), (other_ref, 1 - af)):
        total = jnp.zeros((256, 512), F32)
        for k in range(8):
            source = ha
            for bit, mask in ((1, first), (2, second), (4, third)):
                if k & bit:
                    source = source ^ mask
            w = jnp.concatenate([ref[source, 0], ref[source, 1]], axis=1)
            total = total + dot((near_ref, far_ref)[k // 4][k % 4], w, NT)
        out_ref[:, pl.ds(pl.multiple_of(half * 512, 512), 512)] = total.astype(BF16)


def visual_out(place, mine, other, near, far):
    vmem = pl.BlockSpec(memory_space=pltpu.VMEM)
    return pl.pallas_call(
        visual_kernel,
        in_specs=[pl.BlockSpec(memory_space=pltpu.SMEM)] + [vmem] * 4,
        out_specs=vmem,
        out_shape=jax.ShapeDtypeStruct((256, 1024), BF16),
        compiler_params=pltpu.CompilerParams(vmem_limit_bytes=24 << 20),
        cost_estimate=cost(3),
        name="visual_out",
    )(place, mine, other, near, far)


def swap_cores(a):
    return lax.ppermute(a, "af", [(0, 1), (1, 0)])


def pair(a, axis, masks):
    count = {"pb": 16, "ha": 8}[axis]
    return lax.ppermute(a, (axis, "af"), [(2 * i + c, 2 * (i ^ masks[c]) + c) for i in range(count) for c in range(2)])


def plus(*terms):
    return functools.reduce(jnp.add, [t.astype(F32) for t in terms]).astype(BF16)


def gather_y(a):
    return [a, pair(a, "pb", (4, 12)), pair(a, "pb", (12, 4)), pair(a, "pb", (8, 8))]


def on_device(queries, vis_keys, vis_values, out_grad, key_weight, value_weight, frame_ids, text_mask):
    pb, ha, af = lax.axis_index("pb"), lax.axis_index("ha"), lax.axis_index("af")
    place = jnp.stack([pb // 4, pb % 4, af, ha]).astype(jnp.int32)
    tie = lax.optimization_barrier
    split = lambda w: w.reshape(8, 2, 512, DH)
    qd = jnp.stack([queries, out_grad])
    near, back = pair(qd, "pb", (4, 12)), pair(qd, "pb", (12, 4))
    qt, dt, state, edge, weights = softmax_stats(
        0, text_mask, frame_ids.reshape(VISUAL // 128, 128), qd, vis_keys, vis_values, split(key_weight), split(value_weight)
    )
    state, near, back = tie((state, near, back))
    across = pair(near, "pb", (12, 4))
    stat = softmax_stats(1, vis_keys, vis_values, qt, dt, state, edge)
    stat, across, weights = tie((stat, across, weights))
    stats = jnp.stack(gather_y(stat))
    own = jnp.stack([qd, near, back, across])
    other, stats2 = swap_cores(own), swap_cores(stats)
    weights = lax.all_to_all(weights, "ha", 0, 0, tiled=True)
    part, qsum = visual_token_grads(place, vis_keys, vis_values, edge, own, other, stats, stats2)

    got = pair(part[2:], "pb", (1, 3))
    qpart = plus(qsum[0], swap_cores(qsum[1]))
    got2 = pair(plus(part[1], got[1]), "pb", (3, 1))
    qgot = pair(qpart[2:], "pb", (12, 4))
    g = plus(part[0], got[0], got2)[None]
    qgot2 = pair(plus(qpart[1], qgot[1]), "pb", (4, 12))
    weights2 = swap_cores(weights)
    g = jnp.concatenate([g, pair(g, "ha", (1, 6))], axis=0)
    g = jnp.concatenate([g, pair(g, "ha", (2, 1))], axis=0)
    far = pair(g, "ha", (6, 2))
    query_grad = query_out(plus(qpart[0], qgot[0]), qgot2)
    far, query_grad = tie((far, query_grad))
    visual_grad = visual_out(place, weights, weights2, g, far)
    return query_grad, visual_grad


def solution(mesh):
    in_specs = (
        P("pb", ("ha", "af")),
        P(None, "ha"),
        P(None, "ha"),
        P("pb", ("ha", "af")),
        P(None, "ha"),
        P(None, "ha"),
        P(),
        P("pb", None),
    )
    out_specs = (P("pb", ("ha", "af")), P(("pb", "af"), "ha"))
    return jax.shard_map(on_device, mesh=mesh, in_specs=in_specs, out_specs=out_specs, check_vma=False)
```

```python
import functools

import jax
import jax.numpy as jnp
from jax import lax
from jax.experimental import pallas as pl
from jax.experimental.pallas import tpu as pltpu
from jax.sharding import PartitionSpec as P

DH = 128
FRAMES = 8
QBLK = 32
TOK = 128
ROWS = 512
VISUAL = 8192
PIECE = 256
SUB = 512
TILE = 1024
SCALE = DH**-0.5
C2 = SCALE * 1.4426950408889634
BIG = 2.0**100
VMEM_A = 55
VMEM_B = 24
F32 = jnp.float32
BF16 = jnp.bfloat16
NN = (((1,), (0,)), ((), ()))
NT = (((1,), (1,)), ((), ()))
TN = (((0,), (0,)), ((), ()))


def dot(a, b, dims):
    return lax.dot_general(a, b, dims, preferred_element_type=F32)


def cost(us):
    return pl.CostEstimate(flops=int(us * 1.1e9), transcendentals=0, bytes_accessed=1 << 20)


def marks(base, rows, first, last):
    at = base + lax.broadcasted_iota(jnp.int32, (rows, 128), 0)
    return jnp.where((at >= first) & (at < last), 1.0, 0.0).astype(BF16)


def pieces(x):
    hi = x.astype(BF16).astype(F32)
    rest = x - hi
    mid = rest.astype(BF16).astype(F32)
    return hi, mid, rest - mid


def stat_rows(top, x):
    hi, mid, low = pieces(x)
    row = lax.broadcasted_iota(jnp.int32, top.shape, 0)
    under = jnp.where(row == 0, hi, jnp.where(row == 1, mid, jnp.where(row == 2, low, 0.0)))
    return jnp.concatenate([top, under], axis=0).astype(BF16)


def stats_kernel(
    mask_hbm, fid_hbm, q_hbm, d_hbm, k_hbm, v_hbm, kw_hbm, vw_hbm, own_ref, ka_ref, va_ref, kt_ref, w_hbm,
    mask_ref, fid_ref, k_ref, v_ref, w_ref, qt, dt, sems, wsem, small,
):
    af = lax.axis_index("af")
    smalls = [
        pltpu.make_async_copy(src, dst, small.at[i])
        for i, (src, dst) in enumerate(
            (
                (q_hbm, own_ref.at[0, pl.ds(0, TOK)]),
                (d_hbm, own_ref.at[1, pl.ds(0, TOK)]),
                (fid_hbm, fid_ref),
                (mask_hbm, mask_ref),
            )
        )
    ]
    for copy in smalls:
        copy.start()
    loads = []
    for t in range(VISUAL // TILE):
        at = pl.ds(t * TILE, TILE)
        loads.append(
            [
                pltpu.make_async_copy(k_hbm.at[at], k_ref.at[at], sems.at[0, t]),
                pltpu.make_async_copy(v_hbm.at[at], v_ref.at[at], sems.at[1, t]),
            ]
        )
        for load in loads[t]:
            load.start()
    moves = [pltpu.make_async_copy(w.at[:, af], w_ref.at[i], wsem.at[i]) for i, w in enumerate((kw_hbm, vw_hbm))]
    backs = [pltpu.make_async_copy(w_ref.at[i], w_hbm.at[:, i], wsem.at[2 + i]) for i in range(2)]
    for move in moves:
        move.start()
    for copy in smalls:
        copy.wait()
    fid = fid_ref[...]
    lane = lax.broadcasted_iota(jnp.int32, (8, 128), 1)
    first = jnp.zeros((8, 128), jnp.int32)
    last = jnp.where(lane < 8 + 3, VISUAL, 0)
    for f in range(1, FRAMES):
        below = jnp.sum((fid < f).astype(F32), axis=(0, 1), keepdims=True).astype(jnp.int32)
        first = jnp.where(lane == f, below, first)
        last = jnp.where(lane == f - 1, below, last)
    first, last = first[0:1], last[0:1]
    sub = lax.broadcasted_iota(jnp.int32, (8, 128), 0)
    bias = jnp.zeros((8, 128), F32)
    for b in range(TOK // QBLK):
        for f in range(FRAMES):
            here = (sub == f) & (lane // QBLK == b)
            bias = jnp.where(here, jnp.where(mask_ref[b, f] == 1, 0.0, -BIG), bias)
    top = jnp.concatenate([bias] * 4, axis=1)
    for h in range(4):
        cols = slice(h * DH, (h + 1) * DH)
        qt[:DH, cols] = own_ref[0, :TOK, cols].T
        dt[:, cols] = own_ref[1, :TOK, cols].T
    qt[DH:DH + 16, :] = jnp.concatenate([top, jnp.zeros((8, ROWS), F32)], axis=0).astype(BF16)
    qt[DH + 16:, :] = jnp.zeros((DH - 16, ROWS), BF16)
    m = jnp.full((1, ROWS), -3e38, F32)
    l = jnp.zeros((1, ROWS), F32)
    o = jnp.zeros((DH, ROWS), F32)

    def scores(s):
        if s % (TILE // SUB) == 0:
            for load in loads[s // (TILE // SUB)]:
                load.wait()
        ka = jnp.concatenate([k_ref[s * SUB:(s + 1) * SUB], marks(s * SUB, SUB, first, last)], axis=1)
        return dot(ka, qt[...], NN) * C2

    later = scores(0)
    for s in range(VISUAL // SUB):
        x = later
        m_new = jnp.maximum(m, jnp.max(x, axis=0, keepdims=True))
        if s + 1 < VISUAL // SUB:
            later = scores(s + 1)
        if s == VISUAL // SUB // 2:
            for move, back in zip(moves, backs):
                move.wait()
                back.start()
        shrink = jnp.exp2(m - m_new)
        p = jnp.exp2(x - m_new)
        l = l * shrink + jnp.sum(p, axis=0, keepdims=True)
        o = o * shrink + dot(v_ref[s * SUB:(s + 1) * SUB], p.astype(BF16), TN)
        m = m_new
    y, z = lax.axis_index("pb") // 4, lax.axis_index("pb") % 4
    order = (0, 3 - 2 * af, 1 + 2 * af, 2)
    for s in range(4):
        at = slice(s * PIECE, (s + 1) * PIECE)
        base = y * 2048 + (z ^ order[s]) * 512 + af * 256
        far = pl.ds(pl.multiple_of(base, 256), PIECE)
        mark = marks(base, PIECE, first, last)
        ka_ref[at] = jnp.concatenate([k_ref[far], mark], axis=1)
        va_ref[at] = jnp.concatenate([v_ref[far], mark], axis=1)
        kt_ref[:, at] = k_ref[far].T
    delta = jnp.sum(dt[...].astype(F32) * o, axis=0, keepdims=True) / l
    own_ref[0, TOK:] = stat_rows(top, (m + jnp.log2(l)) * (-1.0 / C2))
    own_ref[1, TOK:] = stat_rows(jnp.zeros((8, ROWS), F32), -delta)
    for back in backs:
        back.wait()


def softmax_stats(*args):
    vmem, far = pl.BlockSpec(memory_space=pltpu.VMEM), pl.BlockSpec(memory_space=pltpu.HBM)
    return pl.pallas_call(
        stats_kernel,
        in_specs=[far] * 8,
        out_specs=[vmem] * 4 + [far],
        out_shape=[
            jax.ShapeDtypeStruct((2, TOK + 16, ROWS), BF16),
            jax.ShapeDtypeStruct((4 * PIECE, 2 * DH), BF16),
            jax.ShapeDtypeStruct((4 * PIECE, 2 * DH), BF16),
            jax.ShapeDtypeStruct((DH, 4 * PIECE), BF16),
            jax.ShapeDtypeStruct((8, 2, 512, DH), BF16),
        ],
        scratch_shapes=[
            pltpu.SMEM((TOK // QBLK, FRAMES), jnp.int32),
            pltpu.VMEM((VISUAL // 128, 128), jnp.int32),
            pltpu.VMEM((VISUAL, DH), BF16),
            pltpu.VMEM((VISUAL, DH), BF16),
            pltpu.VMEM((2, 8, 512, DH), BF16),
            pltpu.VMEM((2 * DH, ROWS), BF16),
            pltpu.VMEM((DH, ROWS), BF16),
            pltpu.SemaphoreType.DMA((2, VISUAL // TILE)),
            pltpu.SemaphoreType.DMA((4,)),
            pltpu.SemaphoreType.DMA((4,)),
        ],
        compiler_params=pltpu.CompilerParams(vmem_limit_bytes=VMEM_A << 20),
        cost_estimate=cost(10),
        name="softmax_stats",
    )(*args)


def grads_kernel(pairs, first_call, last_call, *refs):
    refs = list(refs)
    take = lambda n: [refs.pop(0) for _ in range(n)]
    ka, va, kt = take(3)
    if not first_call:
        ksum_in, vsum_in, *q_in = take(4)
    bundles = take(2 * pairs)
    q_refs = take(2)
    if last_call:
        keep_ref, send_ref = take(2)
    else:
        ksum_out, vsum_out = take(2)
    ksum, vsum = refs
    if not first_call:
        for q_ref, q_old in zip(q_refs, q_in):
            q_ref[0] = q_old[0]
    for block, ref in enumerate(bundles):
        heads = [slice(h * DH, (h + 1) * DH) for h in range(4)]
        empty = jnp.zeros((DH - 16, ROWS), BF16)
        qt, dt = [
            jnp.concatenate(
                [jnp.concatenate([ref[i, :TOK, h].T for h in heads], axis=1), ref[i, TOK:], empty], axis=0
            )
            for i in range(2)
        ]
        qr, dr = [jnp.concatenate([ref[i, :TOK, h] for h in heads], axis=0) for i in range(2)]
        total = jnp.zeros((DH, ROWS), F32)
        final = block == len(bundles) - 1
        for t in range(2):
            at = slice(t * 512, (t + 1) * 512)
            p = jnp.exp2(dot(ka[at], qt, NN) * C2)
            ds = (p * dot(va[at], dt, NN)).astype(BF16)
            kp = dot(ds, qr, NN)
            vp = dot(p.astype(BF16), dr, NN)
            if block or not first_call:
                kp = kp + (ksum if block else ksum_in)[at]
                vp = vp + (vsum if block else vsum_in)[at]
            if not final:
                ksum[at] = kp
                vsum[at] = vp
            elif not last_call:
                ksum_out[at] = kp
                vsum_out[at] = vp
            else:
                for s in range(2):
                    rows = slice(s * PIECE, (s + 1) * PIECE)
                    out = (keep_ref, send_ref)[t]
                    out[s, :, :DH] = (kp[rows] * SCALE).astype(BF16)
                    out[s, :, DH:] = vp[rows].astype(BF16)
            total = total + dot(kt[:, at], ds, NN)
        q_refs[block % 2][block // 2 + (not first_call)] = total.astype(BF16)


def visual_token_grads(name, before, bundles, first_call=False, last_call=False):
    vmem = pl.BlockSpec(memory_space=pltpu.VMEM)
    shape = jax.ShapeDtypeStruct
    outs = [shape((len(bundles) // 2 + (not first_call), DH, ROWS), BF16)] * 2
    outs += [shape((2, PIECE, 2 * DH), BF16)] * 2 if last_call else [shape((4 * PIECE, DH), F32)] * 2
    scratch = [pltpu.VMEM((4 * PIECE, DH), F32)] * 2
    return pl.pallas_call(
        functools.partial(grads_kernel, len(bundles) // 2, first_call, last_call),
        in_specs=[vmem] * (len(before) + len(bundles)),
        out_specs=[vmem] * len(outs),
        out_shape=outs,
        scratch_shapes=scratch,
        compiler_params=pltpu.CompilerParams(vmem_limit_bytes=VMEM_B << 20),
        cost_estimate=cost(1.6 * len(bundles)),
        name=f"visual_token_grads_{name}",
    )(*before, *bundles)


def query_kernel(mine_ref, got_ref, out_ref):
    total = (mine_ref[...].astype(F32) + got_ref[...].astype(F32)) * SCALE
    for h in range(4):
        out_ref[:, h * DH:(h + 1) * DH] = total[:, h * TOK:(h + 1) * TOK].T.astype(BF16)


def query_out(mine, got):
    return pl.pallas_call(
        query_kernel,
        in_specs=[pl.BlockSpec(memory_space=pltpu.VMEM)] * 2,
        out_specs=pl.BlockSpec(memory_space=pltpu.VMEM),
        out_shape=jax.ShapeDtypeStruct((TOK, ROWS), BF16),
        compiler_params=pltpu.CompilerParams(vmem_limit_bytes=4 << 20),
        cost_estimate=cost(1),
        name="query_out",
    )(mine, got)


def visual_kernel(late, place, mine_ref, other_ref, g_ref, *rest):
    sofar_ref, out_ref = rest if late else (None, rest[0])
    af, ha = place[2], place[3]
    first = jnp.where(af == 0, 1, 6)
    second = jnp.where(af == 0, 2, 1)
    third = jnp.where(af == 0, 6, 2)
    totals = []
    for side, ref in enumerate((mine_ref, other_ref)):
        total = sofar_ref[side] if late else jnp.zeros((256, 512), F32)
        for k in range(4):
            source = ha ^ third if late else ha
            for bit, mask in ((1, first), (2, second)):
                if k & bit:
                    source = source ^ mask
            w = jnp.concatenate([ref[source, 0], ref[source, 1]], axis=1)
            total = total + dot(g_ref[k], w, NT)
        if late:
            totals.append(total)
        else:
            out_ref[side] = total
    for core in range(2) if late else ():

        @pl.when(af == core)
        def _():
            for side in range(2):
                at = (side ^ core) * 512
                out_ref[:, at:at + 512] = totals[side].astype(BF16)


def visual_out(place, mine, other, g, *sofar):
    vmem = pl.BlockSpec(memory_space=pltpu.VMEM)
    early = jax.ShapeDtypeStruct((2, 256, 512), F32)
    return pl.pallas_call(
        functools.partial(visual_kernel, bool(sofar)),
        in_specs=[pl.BlockSpec(memory_space=pltpu.SMEM)] + [vmem] * (3 + len(sofar)),
        out_specs=vmem,
        out_shape=jax.ShapeDtypeStruct((256, 1024), BF16) if sofar else early,
        compiler_params=pltpu.CompilerParams(vmem_limit_bytes=24 << 20),
        cost_estimate=cost(2),
        name="visual_late" if sofar else "visual_early",
    )(place, mine, other, g, *sofar)


def swap_cores(a):
    return lax.ppermute(a, "af", [(0, 1), (1, 0)])


def pair(a, axis, masks):
    count = {"pb": 16, "ha": 8}[axis]
    return lax.ppermute(a, (axis, "af"), [(2 * i + c, 2 * (i ^ masks[c]) + c) for i in range(count) for c in range(2)])


def plus(*terms):
    return functools.reduce(jnp.add, [t.astype(F32) for t in terms]).astype(BF16)


def on_device(queries, vis_keys, vis_values, out_grad, key_weight, value_weight, frame_ids, text_mask):
    pb, ha, af = lax.axis_index("pb"), lax.axis_index("ha"), lax.axis_index("af")
    place = jnp.stack([pb // 4, pb % 4, af, ha]).astype(jnp.int32)
    tie = lax.optimization_barrier
    split = lambda w: w.reshape(8, 2, 512, DH)
    own, ka, va, kt, weights = softmax_stats(
        text_mask, frame_ids.reshape(VISUAL // 128, 128), queries, out_grad, vis_keys, vis_values, split(key_weight), split(value_weight)
    )
    weights = lax.all_to_all(weights, "ha", 0, 0, tiled=True)
    near, back = pair(own, "pb", (4, 12)), pair(own, "pb", (12, 4))
    own2 = swap_cores(own)
    early = visual_token_grads("early", [ka, va, kt], [own, own2], first_call=True)
    near, back, early = tie((near, back, early))
    across = pair(near, "pb", (12, 4))
    near2, back2 = swap_cores(near), swap_cores(back)
    qown, qother, keep, send = visual_token_grads(
        "late",
        [ka, va, kt, *early[2:], *early[:2]],
        [near, near2, back, back2, across, swap_cores(across)],
        last_call=True,
    )

    got = pair(send, "pb", (1, 3))
    qpart = plus(qown, swap_cores(qother))
    qgot = pair(qpart[2:], "pb", (12, 4))
    got, qpart = tie((got, qpart))
    got2 = pair(plus(keep[1], got[1]), "pb", (3, 1))
    g = plus(keep[0], got[0], got2)[None]
    weights2 = swap_cores(weights)
    g = jnp.concatenate([g, pair(g, "ha", (1, 6))], axis=0)
    g, qgot = tie((g, qgot))
    qgot2 = pair(plus(qpart[1], qgot[1]), "pb", (4, 12))
    g = jnp.concatenate([g, pair(g, "ha", (2, 1))], axis=0)
    g, qgot2 = tie((g, qgot2))
    far = pair(g, "ha", (6, 2))
    early = visual_out(place, weights, weights2, g)
    query_grad = query_out(plus(qpart[0], qgot[0]), qgot2)
    far, query_grad, early = tie((far, query_grad, early))
    visual_grad = visual_out(place, weights, weights2, far, early)
    return query_grad, visual_grad


def solution(mesh):
    in_specs = (
        P("pb", ("ha", "af")),
        P(None, "ha"),
        P(None, "ha"),
        P("pb", ("ha", "af")),
        P(None, "ha"),
        P(None, "ha"),
        P(),
        P("pb", None),
    )
    out_specs = (P("pb", ("ha", "af")), P(("pb", "af"), "ha"))
    return jax.shard_map(on_device, mesh=mesh, in_specs=in_specs, out_specs=out_specs, check_vma=False)
```

```python
import functools

import jax
import jax.numpy as jnp
from jax import lax
from jax.experimental import pallas as pl
from jax.experimental.pallas import tpu as pltpu
from jax.sharding import PartitionSpec as P

DH = 128
FRAMES = 8
QBLK = 32
TOK = 128
ROWS = 512
VISUAL = 8192
PIECE = 256
SUB = 512
TILE = 1024
SCALE = DH**-0.5
C2 = SCALE * 1.4426950408889634
BIG = 2.0**100
VMEM_A = 55
VMEM_B = 24
F32 = jnp.float32
BF16 = jnp.bfloat16
NN = (((1,), (0,)), ((), ()))
NT = (((1,), (1,)), ((), ()))
TN = (((0,), (0,)), ((), ()))


def dot(a, b, dims):
    return lax.dot_general(a, b, dims, preferred_element_type=F32)


def cost(us):
    return pl.CostEstimate(flops=int(us * 1.1e9), transcendentals=0, bytes_accessed=1 << 20)


def marks(base, rows, first, last):
    at = base + lax.broadcasted_iota(jnp.int32, (rows, 128), 0)
    return jnp.where((at >= first) & (at < last), 1.0, 0.0).astype(BF16)


def pieces(x):
    hi = x.astype(BF16).astype(F32)
    rest = x - hi
    mid = rest.astype(BF16).astype(F32)
    return hi, mid, rest - mid


def stat_rows(top, x):
    hi, mid, low = pieces(x)
    row = lax.broadcasted_iota(jnp.int32, top.shape, 0)
    under = jnp.where(row == 0, hi, jnp.where(row == 1, mid, jnp.where(row == 2, low, 0.0)))
    return jnp.concatenate([top, under], axis=0).astype(BF16)


def stats_kernel(
    mask_hbm, fid_hbm, q_hbm, d_hbm, k_hbm, v_hbm, kw_hbm, vw_hbm, own_ref, ka_hbm, va_hbm, kt_hbm, w_hbm,
    mask_ref, fid_ref, k_ref, v_ref, w_ref, qt, dt, ka_ref, va_ref, kt_ref, sems, wsem, small, osem,
):
    af = lax.axis_index("af")
    smalls = [
        pltpu.make_async_copy(src, dst, small.at[i])
        for i, (src, dst) in enumerate(
            (
                (q_hbm, own_ref.at[0, pl.ds(0, TOK)]),
                (d_hbm, own_ref.at[1, pl.ds(0, TOK)]),
                (fid_hbm, fid_ref),
                (mask_hbm, mask_ref),
            )
        )
    ]
    for copy in smalls:
        copy.start()
    loads = []
    for t in range(VISUAL // TILE):
        at = pl.ds(t * TILE, TILE)
        loads.append(
            [
                pltpu.make_async_copy(k_hbm.at[at], k_ref.at[at], sems.at[0, t]),
                pltpu.make_async_copy(v_hbm.at[at], v_ref.at[at], sems.at[1, t]),
            ]
        )
        for load in loads[t]:
            load.start()
    moves = [pltpu.make_async_copy(w.at[:, af], w_ref.at[i], wsem.at[i]) for i, w in enumerate((kw_hbm, vw_hbm))]
    backs = [pltpu.make_async_copy(w_ref.at[i], w_hbm.at[:, i], wsem.at[2 + i]) for i in range(2)]
    for move in moves:
        move.start()
    for copy in smalls:
        copy.wait()
    fid = fid_ref[...]
    lane = lax.broadcasted_iota(jnp.int32, (8, 128), 1)
    first = jnp.zeros((8, 128), jnp.int32)
    last = jnp.where(lane < 8 + 3, VISUAL, 0)
    for f in range(1, FRAMES):
        below = jnp.sum((fid < f).astype(F32), axis=(0, 1), keepdims=True).astype(jnp.int32)
        first = jnp.where(lane == f, below, first)
        last = jnp.where(lane == f - 1, below, last)
    first, last = first[0:1], last[0:1]
    sub = lax.broadcasted_iota(jnp.int32, (8, 128), 0)
    bias = jnp.zeros((8, 128), F32)
    for b in range(TOK // QBLK):
        for f in range(FRAMES):
            here = (sub == f) & (lane // QBLK == b)
            bias = jnp.where(here, jnp.where(mask_ref[b, f] == 1, 0.0, -BIG), bias)
    top = jnp.concatenate([bias] * 4, axis=1)
    for h in range(4):
        cols = slice(h * DH, (h + 1) * DH)
        qt[:DH, cols] = own_ref[0, :TOK, cols].T
        dt[:, cols] = own_ref[1, :TOK, cols].T
    qt[DH:DH + 16, :] = jnp.concatenate([top, jnp.zeros((8, ROWS), F32)], axis=0).astype(BF16)
    qt[DH + 16:, :] = jnp.zeros((DH - 16, ROWS), BF16)
    m = jnp.full((1, ROWS), -3e38, F32)
    l = jnp.zeros((1, ROWS), F32)
    o = jnp.zeros((DH, ROWS), F32)

    def scores(s):
        if s % (TILE // SUB) == 0:
            for load in loads[s // (TILE // SUB)]:
                load.wait()
        ka = jnp.concatenate([k_ref[s * SUB:(s + 1) * SUB], marks(s * SUB, SUB, first, last)], axis=1)
        return dot(ka, qt[...], NN) * C2

    outs = [
        pltpu.make_async_copy(src, dst, osem.at[i])
        for i, (src, dst) in enumerate(((ka_ref, ka_hbm), (va_ref, va_hbm), (kt_ref, kt_hbm)))
    ]

    def own_tokens():
        y, z = lax.axis_index("pb") // 4, lax.axis_index("pb") % 4
        order = (0, 3 - 2 * af, 1 + 2 * af, 2)
        for s in range(4):
            at = slice(s * PIECE, (s + 1) * PIECE)
            base = y * 2048 + (z ^ order[s]) * 512 + af * 256
            far = pl.ds(pl.multiple_of(base, 256), PIECE)
            mark = marks(base, PIECE, first, last)
            ka_ref[at] = jnp.concatenate([k_ref[far], mark], axis=1)
            va_ref[at] = jnp.concatenate([v_ref[far], mark], axis=1)
            kt_ref[:, at] = k_ref[far].T
        for out in outs:
            out.start()

    later = scores(0)
    for s in range(VISUAL // SUB):
        x = later
        m_new = jnp.maximum(m, jnp.max(x, axis=0, keepdims=True))
        if s + 1 < VISUAL // SUB:
            later = scores(s + 1)
        if s == VISUAL // SUB // 2:
            for move, back in zip(moves, backs):
                move.wait()
                back.start()
        if s == VISUAL // SUB - 3:
            own_tokens()
        shrink = jnp.exp2(m - m_new)
        p = jnp.exp2(x - m_new)
        l = l * shrink + jnp.sum(p, axis=0, keepdims=True)
        o = o * shrink + dot(v_ref[s * SUB:(s + 1) * SUB], p.astype(BF16), TN)
        m = m_new
    delta = jnp.sum(dt[...].astype(F32) * o, axis=0, keepdims=True) / l
    own_ref[0, TOK:] = stat_rows(top, (m + jnp.log2(l)) * (-1.0 / C2))
    own_ref[1, TOK:] = stat_rows(jnp.zeros((8, ROWS), F32), -delta)
    for back in backs + outs:
        back.wait()


def softmax_stats(*args):
    vmem, far = pl.BlockSpec(memory_space=pltpu.VMEM), pl.BlockSpec(memory_space=pltpu.HBM)
    return pl.pallas_call(
        stats_kernel,
        in_specs=[far] * 8,
        out_specs=[vmem] + [far] * 4,
        out_shape=[
            jax.ShapeDtypeStruct((2, TOK + 16, ROWS), BF16),
            jax.ShapeDtypeStruct((4 * PIECE, 2 * DH), BF16),
            jax.ShapeDtypeStruct((4 * PIECE, 2 * DH), BF16),
            jax.ShapeDtypeStruct((DH, 4 * PIECE), BF16),
            jax.ShapeDtypeStruct((8, 2, 512, DH), BF16),
        ],
        scratch_shapes=[
            pltpu.SMEM((TOK // QBLK, FRAMES), jnp.int32),
            pltpu.VMEM((VISUAL // 128, 128), jnp.int32),
            pltpu.VMEM((VISUAL, DH), BF16),
            pltpu.VMEM((VISUAL, DH), BF16),
            pltpu.VMEM((2, 8, 512, DH), BF16),
            pltpu.VMEM((2 * DH, ROWS), BF16),
            pltpu.VMEM((DH, ROWS), BF16),
            pltpu.VMEM((4 * PIECE, 2 * DH), BF16),
            pltpu.VMEM((4 * PIECE, 2 * DH), BF16),
            pltpu.VMEM((DH, 4 * PIECE), BF16),
            pltpu.SemaphoreType.DMA((2, VISUAL // TILE)),
            pltpu.SemaphoreType.DMA((4,)),
            pltpu.SemaphoreType.DMA((4,)),
            pltpu.SemaphoreType.DMA((3,)),
        ],
        compiler_params=pltpu.CompilerParams(vmem_limit_bytes=VMEM_A << 20),
        cost_estimate=cost(10),
        name="softmax_stats",
    )(*args)


def grads_kernel(done, pairs, last_call, *refs):
    first_call = done == 0
    refs = list(refs)
    take = lambda n: [refs.pop(0) for _ in range(n)]
    ka, va, kt = take(3)
    if not first_call:
        ksum_in, vsum_in, *q_in = take(4)
    bundles = take(2 * pairs)
    q_refs = take(2)
    if last_call:
        keep_ref, send_ref = take(2)
    else:
        ksum_out, vsum_out = take(2)
    ksum, vsum = refs
    if not first_call:
        for q_ref, q_old in zip(q_refs, q_in):
            q_ref[:done] = q_old[...]
    for block, ref in enumerate(bundles):
        heads = [slice(h * DH, (h + 1) * DH) for h in range(4)]
        empty = jnp.zeros((DH - 16, ROWS), BF16)
        qt, dt = [
            jnp.concatenate(
                [jnp.concatenate([ref[i, :TOK, h].T for h in heads], axis=1), ref[i, TOK:], empty], axis=0
            )
            for i in range(2)
        ]
        qr, dr = [jnp.concatenate([ref[i, :TOK, h] for h in heads], axis=0) for i in range(2)]
        total = jnp.zeros((DH, ROWS), F32)
        final = block == len(bundles) - 1
        for t in range(2):
            at = slice(t * 512, (t + 1) * 512)
            p = jnp.exp2(dot(ka[at], qt, NN) * C2)
            ds = (p * dot(va[at], dt, NN)).astype(BF16)
            kp = dot(ds, qr, NN)
            vp = dot(p.astype(BF16), dr, NN)
            if block or not first_call:
                kp = kp + (ksum if block else ksum_in)[at]
                vp = vp + (vsum if block else vsum_in)[at]
            if not final:
                ksum[at] = kp
                vsum[at] = vp
            elif not last_call:
                ksum_out[at] = kp
                vsum_out[at] = vp
            else:
                for s in range(2):
                    rows = slice(s * PIECE, (s + 1) * PIECE)
                    out = (keep_ref, send_ref)[t]
                    out[s, :, :DH] = (kp[rows] * SCALE).astype(BF16)
                    out[s, :, DH:] = vp[rows].astype(BF16)
            total = total + dot(kt[:, at], ds, NN)
        q_refs[block % 2][done + block // 2] = total.astype(BF16)


def visual_token_grads(name, before, bundles, done=0, last_call=False):
    vmem = pl.BlockSpec(memory_space=pltpu.VMEM)
    shape = jax.ShapeDtypeStruct
    outs = [shape((done + len(bundles) // 2, DH, ROWS), BF16)] * 2
    outs += [shape((2, PIECE, 2 * DH), BF16)] * 2 if last_call else [shape((4 * PIECE, DH), F32)] * 2
    scratch = [pltpu.VMEM((4 * PIECE, DH), F32)] * 2
    return pl.pallas_call(
        functools.partial(grads_kernel, done, len(bundles) // 2, last_call),
        in_specs=[vmem] * (len(before) + len(bundles)),
        out_specs=[vmem] * len(outs),
        out_shape=outs,
        scratch_shapes=scratch,
        compiler_params=pltpu.CompilerParams(vmem_limit_bytes=VMEM_B << 20),
        cost_estimate=cost(1.6 * len(bundles)),
        name=f"visual_token_grads_{name}",
    )(*before, *bundles)


def query_kernel(mine_ref, got_ref, out_ref):
    total = (mine_ref[...].astype(F32) + got_ref[...].astype(F32)) * SCALE
    for h in range(4):
        out_ref[:, h * DH:(h + 1) * DH] = total[:, h * TOK:(h + 1) * TOK].T.astype(BF16)


def query_out(mine, got):
    return pl.pallas_call(
        query_kernel,
        in_specs=[pl.BlockSpec(memory_space=pltpu.VMEM)] * 2,
        out_specs=pl.BlockSpec(memory_space=pltpu.VMEM),
        out_shape=jax.ShapeDtypeStruct((TOK, ROWS), BF16),
        compiler_params=pltpu.CompilerParams(vmem_limit_bytes=4 << 20),
        cost_estimate=cost(1),
        name="query_out",
    )(mine, got)


def early_kernel(place, mine_ref, other_ref, g_ref, sofar_ref, w_ref):
    af, ha = place[2], place[3]
    first = jnp.where(af == 0, 1, 6)
    second = jnp.where(af == 0, 2, 1)
    third = jnp.where(af == 0, 6, 2)
    for side, ref in enumerate((mine_ref, other_ref)):
        total = jnp.zeros((256, 512), F32)
        for k in range(4):
            source = ha
            for bit, mask in ((1, first), (2, second)):
                if k & bit:
                    source = source ^ mask
            w = jnp.concatenate([ref[source, 0], ref[source, 1]], axis=1)
            total = total + dot(g_ref[k], w, NT)
            for i in range(2):
                w_ref[side, k, :, i * DH:(i + 1) * DH] = ref[source ^ third, i]
        sofar_ref[side] = total


def late_kernel(place, w_ref, g_ref, sofar_ref, out_ref):
    totals = []
    for side in range(2):
        total = sofar_ref[side]
        for k in range(4):
            total = total + dot(g_ref[k], w_ref[side, k], NT)
        totals.append(total)
    for core in range(2):

        @pl.when(place[2] == core)
        def _():
            for side in range(2):
                at = (side ^ core) * 512
                out_ref[:, at:at + 512] = totals[side].astype(BF16)


def visual_call(kernel, name, outs, *args):
    vmem = pl.BlockSpec(memory_space=pltpu.VMEM)
    return pl.pallas_call(
        kernel,
        in_specs=[pl.BlockSpec(memory_space=pltpu.SMEM)] + [vmem] * (len(args) - 1),
        out_specs=[vmem] * len(outs),
        out_shape=outs,
        compiler_params=pltpu.CompilerParams(vmem_limit_bytes=24 << 20),
        cost_estimate=cost(2),
        name=name,
    )(*args)


def visual_early(*args):
    outs = [jax.ShapeDtypeStruct((2, 256, 512), F32), jax.ShapeDtypeStruct((2, 4, 512, 2 * DH), BF16)]
    return visual_call(early_kernel, "visual_early", outs, *args)


def visual_late(*args):
    return visual_call(late_kernel, "visual_late", [jax.ShapeDtypeStruct((256, 1024), BF16)], *args)[0]


def swap_cores(a):
    return lax.ppermute(a, "af", [(0, 1), (1, 0)])


def pair(a, axis, masks):
    count = {"pb": 16, "ha": 8}[axis]
    return lax.ppermute(a, (axis, "af"), [(2 * i + c, 2 * (i ^ masks[c]) + c) for i in range(count) for c in range(2)])


def plus(*terms):
    return functools.reduce(jnp.add, [t.astype(F32) for t in terms]).astype(BF16)


def on_device(queries, vis_keys, vis_values, out_grad, key_weight, value_weight, frame_ids, text_mask):
    pb, ha, af = lax.axis_index("pb"), lax.axis_index("ha"), lax.axis_index("af")
    place = jnp.stack([pb // 4, pb % 4, af, ha]).astype(jnp.int32)
    tie = lax.optimization_barrier
    split = lambda w: w.reshape(8, 2, 512, DH)
    own, ka, va, kt, weights = softmax_stats(
        text_mask, frame_ids.reshape(VISUAL // 128, 128), queries, out_grad, vis_keys, vis_values, split(key_weight), split(value_weight)
    )
    weights = lax.all_to_all(weights, "ha", 0, 0, tiled=True)
    near, back = pair(own, "pb", (4, 12)), pair(own, "pb", (12, 4))
    own2 = swap_cores(own)
    early = visual_token_grads("first", [ka, va, kt], [own, own2])
    near, back, early = tie((near, back, early))
    across = pair(near, "pb", (12, 4))
    middle = visual_token_grads(
        "second", [ka, va, kt, *early[2:], *early[:2]], [near, swap_cores(near), back, swap_cores(back)], done=1
    )
    across, middle = tie((across, middle))
    qown, qother, keep, send = visual_token_grads(
        "third", [ka, va, kt, *middle[2:], *middle[:2]], [across, swap_cores(across)], done=3, last_call=True
    )

    got = pair(send, "pb", (1, 3))
    got, qother = tie((got, qother))
    qpart = plus(qown, swap_cores(qother))
    got2 = pair(plus(keep[1], got[1]), "pb", (3, 1))
    got2, weights, qgot_in = tie((got2, weights, qpart[2:]))
    qgot = pair(qgot_in, "pb", (12, 4))
    g = plus(keep[0], got[0], got2)[None]
    weights2 = swap_cores(weights)
    g = jnp.concatenate([g, pair(g, "ha", (1, 6))], axis=0)
    g, qgot = tie((g, qgot))
    qgot2 = pair(plus(qpart[1], qgot[1]), "pb", (4, 12))
    g = jnp.concatenate([g, pair(g, "ha", (2, 1))], axis=0)
    g, qgot2 = tie((g, qgot2))
    far = pair(g, "ha", (6, 2))
    early, far_weights = visual_early(place, weights, weights2, g)
    query_grad = query_out(plus(qpart[0], qgot[0]), qgot2)
    far, query_grad, early = tie((far, query_grad, early))
    visual_grad = visual_late(place, far_weights, far, early)
    return query_grad, visual_grad


def solution(mesh):
    in_specs = (
        P("pb", ("ha", "af")),
        P(None, "ha"),
        P(None, "ha"),
        P("pb", ("ha", "af")),
        P(None, "ha"),
        P(None, "ha"),
        P(),
        P("pb", None),
    )
    out_specs = (P("pb", ("ha", "af")), P(("pb", "af"), "ha"))
    return jax.shard_map(on_device, mesh=mesh, in_specs=in_specs, out_specs=out_specs, check_vma=False)
```

```python
import functools

import jax
import jax.numpy as jnp
from jax import lax
from jax.experimental import pallas as pl
from jax.experimental.pallas import tpu as pltpu
from jax.sharding import PartitionSpec as P

DH = 128
FRAMES = 8
QBLK = 32
TOK = 128
ROWS = 512
VISUAL = 8192
PIECE = 256
SUB = 1024
TILES = ((0, 1024), (1024, 1024), (2048, 6144))
SCALE = DH**-0.5
C2 = SCALE * 1.4426950408889634
BIG = 2.0**100
VMEM_A = 55
VMEM_B = 24
F32 = jnp.float32
BF16 = jnp.bfloat16
NN = (((1,), (0,)), ((), ()))
NT = (((1,), (1,)), ((), ()))
TN = (((0,), (0,)), ((), ()))


def dot(a, b, dims):
    return lax.dot_general(a, b, dims, preferred_element_type=F32)


def cost(us):
    return pl.CostEstimate(flops=int(us * 1.1e9), transcendentals=0, bytes_accessed=1 << 20)


def marks(base, rows, first, last):
    at = base + lax.broadcasted_iota(jnp.int32, (rows, 128), 0)
    return jnp.where((at >= first) & (at < last), 1.0, 0.0).astype(BF16)


def pieces(x):
    hi = x.astype(BF16).astype(F32)
    rest = x - hi
    mid = rest.astype(BF16).astype(F32)
    return hi, mid, rest - mid


def stat_rows(top, x):
    hi, mid, low = pieces(x)
    row = lax.broadcasted_iota(jnp.int32, top.shape, 0)
    under = jnp.where(row == 0, hi, jnp.where(row == 1, mid, jnp.where(row == 2, low, 0.0)))
    return jnp.concatenate([top, under], axis=0).astype(BF16)


def stats_kernel(
    mask_hbm, fid_hbm, q_hbm, d_hbm, k_hbm, v_hbm, kw_hbm, vw_hbm, own_ref, ka_ref, va_ref, kt_ref, w_hbm,
    mask_ref, fid_ref, k_ref, v_ref, w_ref, qt, dt, sems, wsem, small,
):
    af = lax.axis_index("af")
    smalls = [
        pltpu.make_async_copy(src, dst, small.at[i])
        for i, (src, dst) in enumerate(
            (
                (q_hbm, own_ref.at[0, pl.ds(0, TOK)]),
                (d_hbm, own_ref.at[1, pl.ds(0, TOK)]),
                (fid_hbm, fid_ref),
                (mask_hbm, mask_ref),
            )
        )
    ]
    loads = []
    for t, (start, size) in enumerate(TILES):
        at = pl.ds(start, size)
        loads.append(
            [
                pltpu.make_async_copy(k_hbm.at[at], k_ref.at[at], sems.at[0, t]),
                pltpu.make_async_copy(v_hbm.at[at], v_ref.at[at], sems.at[1, t]),
            ]
        )
        for load in loads[t]:
            load.start()
        if t == 0:
            for copy in smalls:
                copy.start()
    moves = [pltpu.make_async_copy(w.at[:, af], w_ref.at[i], wsem.at[i]) for i, w in enumerate((kw_hbm, vw_hbm))]
    backs = [pltpu.make_async_copy(w_ref.at[i], w_hbm.at[:, i], wsem.at[2 + i]) for i in range(2)]
    for move in moves:
        move.start()
    for copy in smalls:
        copy.wait()
    fid = fid_ref[...]
    lane = lax.broadcasted_iota(jnp.int32, (8, 128), 1)
    first = jnp.zeros((8, 128), jnp.int32)
    last = jnp.where(lane < 8 + 3, VISUAL, 0)
    for f in range(1, FRAMES):
        below = jnp.sum((fid < f).astype(F32), axis=(0, 1), keepdims=True).astype(jnp.int32)
        first = jnp.where(lane == f, below, first)
        last = jnp.where(lane == f - 1, below, last)
    first, last = first[0:1], last[0:1]
    sub = lax.broadcasted_iota(jnp.int32, (8, 128), 0)
    bias = jnp.zeros((8, 128), F32)
    for b in range(TOK // QBLK):
        for f in range(FRAMES):
            here = (sub == f) & (lane // QBLK == b)
            bias = jnp.where(here, jnp.where(mask_ref[b, f] == 1, 0.0, -BIG), bias)
    top = jnp.concatenate([bias] * 4, axis=1)
    for h in range(4):
        cols = slice(h * DH, (h + 1) * DH)
        qt[:DH, cols] = own_ref[0, :TOK, cols].T
        dt[:, cols] = own_ref[1, :TOK, cols].T
    qt[DH:DH + 16, :] = jnp.concatenate([top, jnp.zeros((8, ROWS), F32)], axis=0).astype(BF16)
    qt[DH + 16:, :] = jnp.zeros((DH - 16, ROWS), BF16)
    m = jnp.full((1, ROWS), -3e38, F32)
    l = jnp.zeros((1, ROWS), F32)
    o = jnp.zeros((DH, ROWS), F32)

    def scores(s):
        for (start, _), waits in zip(TILES, loads):
            if start == s * SUB:
                for load in waits:
                    load.wait()
        ka = jnp.concatenate([k_ref[s * SUB:(s + 1) * SUB], marks(s * SUB, SUB, first, last)], axis=1)
        return dot(ka, qt[...], NN) * C2

    later = scores(0)
    for s in range(VISUAL // SUB):
        x = later
        m_new = jnp.maximum(m, jnp.max(x, axis=0, keepdims=True))
        if s + 1 < VISUAL // SUB:
            later = scores(s + 1)
        if s == VISUAL // SUB // 2:
            for move, back in zip(moves, backs):
                move.wait()
                back.start()
        shrink = jnp.exp2(m - m_new)
        p = jnp.exp2(x - m_new)
        l = l * shrink + jnp.sum(p, axis=0, keepdims=True)
        o = o * shrink + dot(v_ref[s * SUB:(s + 1) * SUB], p.astype(BF16), TN)
        m = m_new
    y, z = lax.axis_index("pb") // 4, lax.axis_index("pb") % 4
    order = (0, 3 - 2 * af, 1 + 2 * af, 2)
    for s in range(4):
        at = slice(s * PIECE, (s + 1) * PIECE)
        base = y * 2048 + (z ^ order[s]) * 512 + af * 256
        far = pl.ds(pl.multiple_of(base, 256), PIECE)
        mark = marks(base, PIECE, first, last)
        ka_ref[at] = jnp.concatenate([k_ref[far], mark], axis=1)
        va_ref[at] = jnp.concatenate([v_ref[far], mark], axis=1)
        kt_ref[:, at] = k_ref[far].T
    delta = jnp.sum(dt[...].astype(F32) * o, axis=0, keepdims=True) / l
    own_ref[0, TOK:] = stat_rows(top, (m + jnp.log2(l)) * (-1.0 / C2))
    own_ref[1, TOK:] = stat_rows(jnp.zeros((8, ROWS), F32), -delta)
    for back in backs:
        back.wait()


def softmax_stats(*args):
    vmem, far = pl.BlockSpec(memory_space=pltpu.VMEM), pl.BlockSpec(memory_space=pltpu.HBM)
    return pl.pallas_call(
        stats_kernel,
        in_specs=[far] * 8,
        out_specs=[vmem] * 4 + [far],
        out_shape=[
            jax.ShapeDtypeStruct((2, TOK + 16, ROWS), BF16),
            jax.ShapeDtypeStruct((4 * PIECE, 2 * DH), BF16),
            jax.ShapeDtypeStruct((4 * PIECE, 2 * DH), BF16),
            jax.ShapeDtypeStruct((DH, 4 * PIECE), BF16),
            jax.ShapeDtypeStruct((8, 2, 512, DH), BF16),
        ],
        scratch_shapes=[
            pltpu.SMEM((TOK // QBLK, FRAMES), jnp.int32),
            pltpu.VMEM((VISUAL // 128, 128), jnp.int32),
            pltpu.VMEM((VISUAL, DH), BF16),
            pltpu.VMEM((VISUAL, DH), BF16),
            pltpu.VMEM((2, 8, 512, DH), BF16),
            pltpu.VMEM((2 * DH, ROWS), BF16),
            pltpu.VMEM((DH, ROWS), BF16),
            pltpu.SemaphoreType.DMA((2, len(TILES))),
            pltpu.SemaphoreType.DMA((4,)),
            pltpu.SemaphoreType.DMA((4,)),
        ],
        compiler_params=pltpu.CompilerParams(vmem_limit_bytes=VMEM_A << 20),
        cost_estimate=cost(10),
        name="softmax_stats",
    )(*args)


def grads_kernel(done, pairs, last_call, *refs):
    first_call = done == 0
    refs = list(refs)
    take = lambda n: [refs.pop(0) for _ in range(n)]
    ka, va, kt = take(3)
    if not first_call:
        ksum_in, vsum_in, *q_in = take(4)
    bundles = take(2 * pairs)
    q_refs = take(2)
    if last_call:
        keep_ref, send_ref = take(2)
    else:
        ksum_out, vsum_out = take(2)
    ksum, vsum = refs
    if not first_call:
        for q_ref, q_old in zip(q_refs, q_in):
            q_ref[:done] = q_old[...]
    for block, ref in enumerate(bundles):
        heads = [slice(h * DH, (h + 1) * DH) for h in range(4)]
        empty = jnp.zeros((DH - 16, ROWS), BF16)
        qt, dt = [
            jnp.concatenate(
                [jnp.concatenate([ref[i, :TOK, h].T for h in heads], axis=1), ref[i, TOK:], empty], axis=0
            )
            for i in range(2)
        ]
        qr, dr = [jnp.concatenate([ref[i, :TOK, h] for h in heads], axis=0) for i in range(2)]
        total = jnp.zeros((DH, ROWS), F32)
        final = block == len(bundles) - 1
        for t in range(2):
            at = slice(t * 512, (t + 1) * 512)
            p = jnp.exp2(dot(ka[at], qt, NN) * C2)
            ds = (p * dot(va[at], dt, NN)).astype(BF16)
            kp = dot(ds, qr, NN)
            vp = dot(p.astype(BF16), dr, NN)
            if block or not first_call:
                kp = kp + (ksum if block else ksum_in)[at]
                vp = vp + (vsum if block else vsum_in)[at]
            if not final:
                ksum[at] = kp
                vsum[at] = vp
            elif not last_call:
                ksum_out[at] = kp
                vsum_out[at] = vp
            else:
                for s in range(2):
                    rows = slice(s * PIECE, (s + 1) * PIECE)
                    out = (keep_ref, send_ref)[t]
                    out[s, :, :DH] = (kp[rows] * SCALE).astype(BF16)
                    out[s, :, DH:] = vp[rows].astype(BF16)
            total = total + dot(kt[:, at], ds, NN)
        q_refs[block % 2][done + block // 2] = total.astype(BF16)


def visual_token_grads(name, before, bundles, done=0, last_call=False):
    vmem = pl.BlockSpec(memory_space=pltpu.VMEM)
    shape = jax.ShapeDtypeStruct
    outs = [shape((done + len(bundles) // 2, DH, ROWS), BF16)] * 2
    outs += [shape((2, PIECE, 2 * DH), BF16)] * 2 if last_call else [shape((4 * PIECE, DH), F32)] * 2
    scratch = [pltpu.VMEM((4 * PIECE, DH), F32)] * 2
    return pl.pallas_call(
        functools.partial(grads_kernel, done, len(bundles) // 2, last_call),
        in_specs=[vmem] * (len(before) + len(bundles)),
        out_specs=[vmem] * len(outs),
        out_shape=outs,
        scratch_shapes=scratch,
        compiler_params=pltpu.CompilerParams(vmem_limit_bytes=VMEM_B << 20),
        cost_estimate=cost(1.6 * len(bundles)),
        name=f"visual_token_grads_{name}",
    )(*before, *bundles)


def query_kernel(mine_ref, got_ref, out_ref):
    total = (mine_ref[...].astype(F32) + got_ref[...].astype(F32)) * SCALE
    for h in range(4):
        out_ref[:, h * DH:(h + 1) * DH] = total[:, h * TOK:(h + 1) * TOK].T.astype(BF16)


def query_out(mine, got):
    return pl.pallas_call(
        query_kernel,
        in_specs=[pl.BlockSpec(memory_space=pltpu.VMEM)] * 2,
        out_specs=pl.BlockSpec(memory_space=pltpu.VMEM),
        out_shape=jax.ShapeDtypeStruct((TOK, ROWS), BF16),
        compiler_params=pltpu.CompilerParams(vmem_limit_bytes=4 << 20),
        cost_estimate=cost(1),
        name="query_out",
    )(mine, got)


def early_kernel(place, mine_ref, other_ref, g_ref, sofar_ref, w_ref):
    af, ha = place[2], place[3]
    first = jnp.where(af == 0, 1, 6)
    second = jnp.where(af == 0, 2, 1)
    third = jnp.where(af == 0, 6, 2)
    for side, ref in enumerate((mine_ref, other_ref)):
        total = jnp.zeros((256, 512), F32)
        for k in range(4):
            source = ha
            for bit, mask in ((1, first), (2, second)):
                if k & bit:
                    source = source ^ mask
            w = jnp.concatenate([ref[source, 0], ref[source, 1]], axis=1)
            total = total + dot(g_ref[k], w, NT)
            for i in range(2):
                w_ref[side, k, :, i * DH:(i + 1) * DH] = ref[source ^ third, i]
        sofar_ref[side] = total


def late_kernel(place, w_ref, g_ref, sofar_ref, out_ref):
    totals = []
    for side in range(2):
        total = sofar_ref[side]
        for k in range(4):
            total = total + dot(g_ref[k], w_ref[side, k], NT)
        totals.append(total)
    for core in range(2):

        @pl.when(place[2] == core)
        def _():
            for side in range(2):
                at = (side ^ core) * 512
                out_ref[:, at:at + 512] = totals[side].astype(BF16)


def visual_call(kernel, name, outs, *args):
    vmem = pl.BlockSpec(memory_space=pltpu.VMEM)
    return pl.pallas_call(
        kernel,
        in_specs=[pl.BlockSpec(memory_space=pltpu.SMEM)] + [vmem] * (len(args) - 1),
        out_specs=[vmem] * len(outs),
        out_shape=outs,
        compiler_params=pltpu.CompilerParams(vmem_limit_bytes=24 << 20),
        cost_estimate=cost(2),
        name=name,
    )(*args)


def visual_early(*args):
    outs = [jax.ShapeDtypeStruct((2, 256, 512), F32), jax.ShapeDtypeStruct((2, 4, 512, 2 * DH), BF16)]
    return visual_call(early_kernel, "visual_early", outs, *args)


def visual_late(*args):
    return visual_call(late_kernel, "visual_late", [jax.ShapeDtypeStruct((256, 1024), BF16)], *args)[0]


def swap_cores(a):
    return lax.ppermute(a, "af", [(0, 1), (1, 0)])


def pair(a, axis, masks):
    count = {"pb": 16, "ha": 8}[axis]
    return lax.ppermute(a, (axis, "af"), [(2 * i + c, 2 * (i ^ masks[c]) + c) for i in range(count) for c in range(2)])


def plus(*terms):
    return functools.reduce(jnp.add, [t.astype(F32) for t in terms]).astype(BF16)


def on_device(queries, vis_keys, vis_values, out_grad, key_weight, value_weight, frame_ids, text_mask):
    pb, ha, af = lax.axis_index("pb"), lax.axis_index("ha"), lax.axis_index("af")
    place = jnp.stack([pb // 4, pb % 4, af, ha]).astype(jnp.int32)
    tie = lax.optimization_barrier
    split = lambda w: w.reshape(8, 2, 512, DH)
    own, ka, va, kt, weights = softmax_stats(
        text_mask, frame_ids.reshape(VISUAL // 128, 128), queries, out_grad, vis_keys, vis_values, split(key_weight), split(value_weight)
    )
    weights = lax.all_to_all(weights, "ha", 0, 0, tiled=True)
    near, back = pair(own, "pb", (4, 12)), pair(own, "pb", (12, 4))
    own2 = swap_cores(own)
    early = visual_token_grads("first", [ka, va, kt], [own, own2])
    near, back, early = tie((near, back, early))
    across = pair(near, "pb", (12, 4))
    middle = visual_token_grads(
        "second", [ka, va, kt, *early[2:], *early[:2]], [near, swap_cores(near), back, swap_cores(back)], done=1
    )
    across, middle = tie((across, middle))
    qown, qother, keep, send = visual_token_grads(
        "third", [ka, va, kt, *middle[2:], *middle[:2]], [across, swap_cores(across)], done=3, last_call=True
    )

    got = pair(send, "pb", (1, 3))
    got, qother = tie((got, qother))
    qpart = plus(qown, swap_cores(qother))
    got2 = pair(plus(keep[1], got[1]), "pb", (3, 1))
    got2, weights, qgot_in = tie((got2, weights, qpart[2:]))
    qgot = pair(qgot_in, "pb", (12, 4))
    g = plus(keep[0], got[0], got2)[None]
    weights2 = swap_cores(weights)
    g = jnp.concatenate([g, pair(g, "ha", (1, 6))], axis=0)
    g, qgot = tie((g, qgot))
    qgot2 = pair(plus(qpart[1], qgot[1]), "pb", (4, 12))
    g = jnp.concatenate([g, pair(g, "ha", (2, 1))], axis=0)
    g, qgot2 = tie((g, qgot2))
    far = pair(g, "ha", (6, 2))
    early, far_weights = visual_early(place, weights, weights2, g)
    query_grad = query_out(plus(qpart[0], qgot[0]), qgot2)
    far, query_grad, early = tie((far, query_grad, early))
    visual_grad = visual_late(place, far_weights, far, early)
    return query_grad, visual_grad


def solution(mesh):
    in_specs = (
        P("pb", ("ha", "af")),
        P(None, "ha"),
        P(None, "ha"),
        P("pb", ("ha", "af")),
        P(None, "ha"),
        P(None, "ha"),
        P(),
        P("pb", None),
    )
    out_specs = (P("pb", ("ha", "af")), P(("pb", "af"), "ha"))
    return jax.shard_map(on_device, mesh=mesh, in_specs=in_specs, out_specs=out_specs, check_vma=False)
```

```python
import functools

import jax
import jax.numpy as jnp
from jax import lax
from jax.experimental import pallas as pl
from jax.experimental.pallas import tpu as pltpu
from jax.sharding import PartitionSpec as P

DH = 128
FRAMES = 8
QBLK = 32
TOK = 128
ROWS = 512
VISUAL = 8192
PIECE = 256
SUB = 1024
TILES = ((0, 1024), (1024, 1024), (2048, 6144))
SCALE = DH**-0.5
C2 = SCALE * 1.4426950408889634
BIG = 2.0**100
VMEM_A = 55
VMEM_B = 24
F32 = jnp.float32
BF16 = jnp.bfloat16
NN = (((1,), (0,)), ((), ()))
NT = (((1,), (1,)), ((), ()))
TN = (((0,), (0,)), ((), ()))


def dot(a, b, dims):
    return lax.dot_general(a, b, dims, preferred_element_type=F32)


def cost(us):
    return pl.CostEstimate(flops=int(us * 1.1e9), transcendentals=0, bytes_accessed=1 << 20)


def marks(base, rows, first, last):
    at = base + lax.broadcasted_iota(jnp.int32, (rows, 128), 0)
    return jnp.where((at >= first) & (at < last), 1.0, 0.0).astype(BF16)


def pieces(x):
    hi = x.astype(BF16).astype(F32)
    rest = x - hi
    mid = rest.astype(BF16).astype(F32)
    return hi, mid, rest - mid


def stat_rows(top, x):
    hi, mid, low = pieces(x)
    row = lax.broadcasted_iota(jnp.int32, top.shape, 0)
    under = jnp.where(row == 0, hi, jnp.where(row == 1, mid, jnp.where(row == 2, low, 0.0)))
    return jnp.concatenate([top, under], axis=0).astype(BF16)


def stats_kernel(
    mask_hbm, fid_hbm, q_hbm, d_hbm, k_hbm, v_hbm, kw_hbm, vw_hbm, own_ref, ka_ref, va_ref, kt_ref, w_hbm,
    mask_ref, fid_ref, k_ref, v_ref, w_ref, qt, dt, sems, wsem, small,
):
    af = lax.axis_index("af")
    smalls = [
        pltpu.make_async_copy(src, dst, small.at[i])
        for i, (src, dst) in enumerate(
            (
                (q_hbm, own_ref.at[0, pl.ds(0, TOK)]),
                (d_hbm, own_ref.at[1, pl.ds(0, TOK)]),
                (fid_hbm, fid_ref),
                (mask_hbm, mask_ref),
            )
        )
    ]
    loads = []
    for t, (start, size) in enumerate(TILES):
        at = pl.ds(start, size)
        loads.append(
            [
                pltpu.make_async_copy(k_hbm.at[at], k_ref.at[at], sems.at[0, t]),
                pltpu.make_async_copy(v_hbm.at[at], v_ref.at[at], sems.at[1, t]),
            ]
        )
        for load in loads[t]:
            load.start()
        if t == 0:
            for copy in smalls:
                copy.start()
    moves = [pltpu.make_async_copy(w.at[:, af], w_ref.at[i], wsem.at[i]) for i, w in enumerate((kw_hbm, vw_hbm))]
    backs = [pltpu.make_async_copy(w_ref.at[i], w_hbm.at[:, i], wsem.at[2 + i]) for i in range(2)]
    for move in moves:
        move.start()
    for copy in smalls:
        copy.wait()
    fid = fid_ref[...]
    lane = lax.broadcasted_iota(jnp.int32, (8, 128), 1)
    first = jnp.zeros((8, 128), jnp.int32)
    last = jnp.where(lane < 8 + 3, VISUAL, 0)
    for f in range(1, FRAMES):
        below = jnp.sum((fid < f).astype(F32), axis=(0, 1), keepdims=True).astype(jnp.int32)
        first = jnp.where(lane == f, below, first)
        last = jnp.where(lane == f - 1, below, last)
    first, last = first[0:1], last[0:1]
    sub = lax.broadcasted_iota(jnp.int32, (8, 128), 0)
    bias = jnp.zeros((8, 128), F32)
    for b in range(TOK // QBLK):
        for f in range(FRAMES):
            here = (sub == f) & (lane // QBLK == b)
            bias = jnp.where(here, jnp.where(mask_ref[b, f] == 1, 0.0, -BIG), bias)
    top = jnp.concatenate([bias] * 4, axis=1)
    for h in range(4):
        cols = slice(h * DH, (h + 1) * DH)
        qt[:DH, cols] = own_ref[0, :TOK, cols].T
        dt[:, cols] = own_ref[1, :TOK, cols].T
    qt[DH:DH + 16, :] = jnp.concatenate([top, jnp.zeros((8, ROWS), F32)], axis=0).astype(BF16)
    qt[DH + 16:, :] = jnp.zeros((DH - 16, ROWS), BF16)
    m = jnp.full((1, ROWS), -3e38, F32)
    l = jnp.zeros((1, ROWS), F32)
    o = jnp.zeros((DH, ROWS), F32)

    def scores(s):
        for (start, _), waits in zip(TILES, loads):
            if start == s * SUB:
                for load in waits:
                    load.wait()
        ka = jnp.concatenate([k_ref[s * SUB:(s + 1) * SUB], marks(s * SUB, SUB, first, last)], axis=1)
        return dot(ka, qt[...], NN) * C2

    later = scores(0)
    for s in range(VISUAL // SUB):
        x = later
        m_new = jnp.maximum(m, jnp.max(x, axis=0, keepdims=True))
        if s + 1 < VISUAL // SUB:
            later = scores(s + 1)
        if s == VISUAL // SUB // 2:
            for move, back in zip(moves, backs):
                move.wait()
                back.start()
        shrink = jnp.exp2(m - m_new)
        p = jnp.exp2(x - m_new)
        l = l * shrink + jnp.sum(p, axis=0, keepdims=True)
        o = o * shrink + dot(v_ref[s * SUB:(s + 1) * SUB], p.astype(BF16), TN)
        m = m_new
    y, z = lax.axis_index("pb") // 4, lax.axis_index("pb") % 4
    order = (0, 3 - 2 * af, 1 + 2 * af, 2)
    for s in range(4):
        at = slice(s * PIECE, (s + 1) * PIECE)
        base = y * 2048 + (z ^ order[s]) * 512 + af * 256
        far = pl.ds(pl.multiple_of(base, 256), PIECE)
        mark = marks(base, PIECE, first, last)
        ka_ref[at] = jnp.concatenate([k_ref[far], mark], axis=1)
        va_ref[at] = jnp.concatenate([v_ref[far], mark], axis=1)
        kt_ref[:, at] = k_ref[far].T
    delta = jnp.sum(dt[...].astype(F32) * o, axis=0, keepdims=True) / l
    own_ref[0, TOK:] = stat_rows(top, (m + jnp.log2(l)) * (-1.0 / C2))
    own_ref[1, TOK:] = stat_rows(jnp.zeros((8, ROWS), F32), -delta)
    for back in backs:
        back.wait()


def softmax_stats(*args):
    vmem, far = pl.BlockSpec(memory_space=pltpu.VMEM), pl.BlockSpec(memory_space=pltpu.HBM)
    return pl.pallas_call(
        stats_kernel,
        in_specs=[far] * 8,
        out_specs=[vmem] * 4 + [far],
        out_shape=[
            jax.ShapeDtypeStruct((2, TOK + 16, ROWS), BF16),
            jax.ShapeDtypeStruct((4 * PIECE, 2 * DH), BF16),
            jax.ShapeDtypeStruct((4 * PIECE, 2 * DH), BF16),
            jax.ShapeDtypeStruct((DH, 4 * PIECE), BF16),
            jax.ShapeDtypeStruct((8, 2, 512, DH), BF16),
        ],
        scratch_shapes=[
            pltpu.SMEM((TOK // QBLK, FRAMES), jnp.int32),
            pltpu.VMEM((VISUAL // 128, 128), jnp.int32),
            pltpu.VMEM((VISUAL, DH), BF16),
            pltpu.VMEM((VISUAL, DH), BF16),
            pltpu.VMEM((2, 8, 512, DH), BF16),
            pltpu.VMEM((2 * DH, ROWS), BF16),
            pltpu.VMEM((DH, ROWS), BF16),
            pltpu.SemaphoreType.DMA((2, len(TILES))),
            pltpu.SemaphoreType.DMA((4,)),
            pltpu.SemaphoreType.DMA((4,)),
        ],
        compiler_params=pltpu.CompilerParams(vmem_limit_bytes=VMEM_A << 20),
        cost_estimate=cost(10),
        name="softmax_stats",
    )(*args)


def grads_kernel(done, pairs, last_call, *refs):
    first_call = done == 0
    refs = list(refs)
    take = lambda n: [refs.pop(0) for _ in range(n)]
    ka, va, kt = take(3)
    if not first_call:
        ksum_in, vsum_in, *q_in = take(4)
    bundles = take(2 * pairs)
    q_refs = take(2)
    if last_call:
        keep_ref, send_ref = take(2)
    else:
        ksum_out, vsum_out = take(2)
    ksum, vsum = refs
    if not first_call:
        for q_ref, q_old in zip(q_refs, q_in):
            q_ref[:done] = q_old[...]
    for block, ref in enumerate(bundles):
        heads = [slice(h * DH, (h + 1) * DH) for h in range(4)]
        empty = jnp.zeros((DH - 16, ROWS), BF16)
        qt, dt = [
            jnp.concatenate(
                [jnp.concatenate([ref[i, :TOK, h].T for h in heads], axis=1), ref[i, TOK:], empty], axis=0
            )
            for i in range(2)
        ]
        qr, dr = [jnp.concatenate([ref[i, :TOK, h] for h in heads], axis=0) for i in range(2)]
        total = jnp.zeros((DH, ROWS), F32)
        final = block == len(bundles) - 1
        for t in range(2):
            at = slice(t * 512, (t + 1) * 512)
            p = jnp.exp2(dot(ka[at], qt, NN) * C2)
            ds = (p * dot(va[at], dt, NN)).astype(BF16)
            kp = dot(ds, qr, NN)
            vp = dot(p.astype(BF16), dr, NN)
            if block or not first_call:
                kp = kp + (ksum if block else ksum_in)[at]
                vp = vp + (vsum if block else vsum_in)[at]
            if not final:
                ksum[at] = kp
                vsum[at] = vp
            elif not last_call:
                ksum_out[at] = kp
                vsum_out[at] = vp
            else:
                for s in range(2):
                    rows = slice(s * PIECE, (s + 1) * PIECE)
                    out = (keep_ref, send_ref)[t]
                    out[s, :, :DH] = (kp[rows] * SCALE).astype(BF16)
                    out[s, :, DH:] = vp[rows].astype(BF16)
            total = total + dot(kt[:, at], ds, NN)
        q_refs[block % 2][done + block // 2] = total.astype(BF16)


def visual_token_grads(name, before, bundles, done=0, last_call=False):
    vmem = pl.BlockSpec(memory_space=pltpu.VMEM)
    shape = jax.ShapeDtypeStruct
    outs = [shape((done + len(bundles) // 2, DH, ROWS), BF16)] * 2
    outs += [shape((2, PIECE, 2 * DH), BF16)] * 2 if last_call else [shape((4 * PIECE, DH), F32)] * 2
    scratch = [pltpu.VMEM((4 * PIECE, DH), F32)] * 2
    return pl.pallas_call(
        functools.partial(grads_kernel, done, len(bundles) // 2, last_call),
        in_specs=[vmem] * (len(before) + len(bundles)),
        out_specs=[vmem] * len(outs),
        out_shape=outs,
        scratch_shapes=scratch,
        compiler_params=pltpu.CompilerParams(vmem_limit_bytes=VMEM_B << 20),
        cost_estimate=cost(1.6 * len(bundles)),
        name=f"visual_token_grads_{name}",
    )(*before, *bundles)


def query_kernel(mine_ref, got_ref, out_ref):
    total = (mine_ref[...].astype(F32) + got_ref[...].astype(F32)) * SCALE
    for h in range(4):
        out_ref[:, h * DH:(h + 1) * DH] = total[:, h * TOK:(h + 1) * TOK].T.astype(BF16)


def query_out(mine, got):
    return pl.pallas_call(
        query_kernel,
        in_specs=[pl.BlockSpec(memory_space=pltpu.VMEM)] * 2,
        out_specs=pl.BlockSpec(memory_space=pltpu.VMEM),
        out_shape=jax.ShapeDtypeStruct((TOK, ROWS), BF16),
        compiler_params=pltpu.CompilerParams(vmem_limit_bytes=4 << 20),
        cost_estimate=cost(1),
        name="query_out",
    )(mine, got)


def early_kernel(place, mine_ref, other_ref, g_ref, sofar_ref, w_ref):
    af, ha = place[2], place[3]
    first = jnp.where(af == 0, 1, 6)
    second = jnp.where(af == 0, 2, 1)
    third = jnp.where(af == 0, 6, 2)
    for side, ref in enumerate((mine_ref, other_ref)):
        total = jnp.zeros((256, 512), F32)
        for k in range(4):
            source = ha
            for bit, mask in ((1, first), (2, second)):
                if k & bit:
                    source = source ^ mask
            w = jnp.concatenate([ref[source, 0], ref[source, 1]], axis=1)
            total = total + dot(g_ref[k], w, NT)
            for i in range(2):
                w_ref[side, k, :, i * DH:(i + 1) * DH] = ref[source ^ third, i]
        sofar_ref[side] = total


def late_kernel(place, w_ref, g_ref, sofar_ref, out_ref):
    totals = []
    for side in range(2):
        total = sofar_ref[side]
        for k in range(4):
            total = total + dot(g_ref[k], w_ref[side, k], NT)
        totals.append(total)
    for core in range(2):

        @pl.when(place[2] == core)
        def _():
            for side in range(2):
                at = (side ^ core) * 512
                out_ref[:, at:at + 512] = totals[side].astype(BF16)


def visual_call(kernel, name, outs, *args):
    vmem = pl.BlockSpec(memory_space=pltpu.VMEM)
    return pl.pallas_call(
        kernel,
        in_specs=[pl.BlockSpec(memory_space=pltpu.SMEM)] + [vmem] * (len(args) - 1),
        out_specs=[vmem] * len(outs),
        out_shape=outs,
        compiler_params=pltpu.CompilerParams(vmem_limit_bytes=24 << 20),
        cost_estimate=cost(2),
        name=name,
    )(*args)


def visual_early(*args):
    outs = [jax.ShapeDtypeStruct((2, 256, 512), F32), jax.ShapeDtypeStruct((2, 4, 512, 2 * DH), BF16)]
    return visual_call(early_kernel, "visual_early", outs, *args)


def visual_late(*args):
    return visual_call(late_kernel, "visual_late", [jax.ShapeDtypeStruct((256, 1024), BF16)], *args)[0]


def swap_cores(a):
    return lax.ppermute(a, "af", [(0, 1), (1, 0)])


def pair(a, axis, masks):
    count = {"pb": 16, "ha": 8}[axis]
    return lax.ppermute(a, (axis, "af"), [(2 * i + c, 2 * (i ^ masks[c]) + c) for i in range(count) for c in range(2)])


def plus(*terms):
    return functools.reduce(jnp.add, [t.astype(F32) for t in terms]).astype(BF16)


def on_device(queries, vis_keys, vis_values, out_grad, key_weight, value_weight, frame_ids, text_mask):
    pb, ha, af = lax.axis_index("pb"), lax.axis_index("ha"), lax.axis_index("af")
    place = jnp.stack([pb // 4, pb % 4, af, ha]).astype(jnp.int32)
    tie = lax.optimization_barrier
    split = lambda w: w.reshape(8, 2, 512, DH)
    own, ka, va, kt, weights = softmax_stats(
        text_mask, frame_ids.reshape(VISUAL // 128, 128), queries, out_grad, vis_keys, vis_values, split(key_weight), split(value_weight)
    )
    weights = lax.all_to_all(weights, "ha", 0, 0, tiled=True)
    near, back = pair(own, "pb", (4, 12)), pair(own, "pb", (12, 4))
    own2 = swap_cores(own)
    early = visual_token_grads("first", [ka, va, kt], [own, own2])
    near, back, early = tie((near, back, early))
    across = pair(near, "pb", (12, 4))
    middle = visual_token_grads(
        "second", [ka, va, kt, *early[2:], *early[:2]], [near, swap_cores(near), back, swap_cores(back)], done=1
    )
    across, middle = tie((across, middle))
    qown, qother, keep, send = visual_token_grads(
        "third", [ka, va, kt, *middle[2:], *middle[:2]], [across, swap_cores(across)], done=3, last_call=True
    )

    got = pair(send, "pb", (1, 3))
    got, qother = tie((got, qother))
    qpart = plus(qown, swap_cores(qother))
    got2 = pair(plus(keep[1], got[1]), "pb", (3, 1))
    got2, qgot_in = tie((got2, qpart[2:]))
    qgot = pair(qgot_in, "pb", (12, 4))
    g = plus(keep[0], got[0], got2)[None]
    g = jnp.concatenate([g, pair(g, "ha", (1, 6))], axis=0)
    g, qgot, weights = tie((g, qgot, weights))
    weights2 = swap_cores(weights)
    qgot2 = pair(plus(qpart[1], qgot[1]), "pb", (4, 12))
    g = jnp.concatenate([g, pair(g, "ha", (2, 1))], axis=0)
    g, qgot2 = tie((g, qgot2))
    far = pair(g, "ha", (6, 2))
    early, far_weights = visual_early(place, weights, weights2, g)
    query_grad = query_out(plus(qpart[0], qgot[0]), qgot2)
    far, query_grad, early = tie((far, query_grad, early))
    visual_grad = visual_late(place, far_weights, far, early)
    return query_grad, visual_grad


def solution(mesh):
    in_specs = (
        P("pb", ("ha", "af")),
        P(None, "ha"),
        P(None, "ha"),
        P("pb", ("ha", "af")),
        P(None, "ha"),
        P(None, "ha"),
        P(),
        P("pb", None),
    )
    out_specs = (P("pb", ("ha", "af")), P(("pb", "af"), "ha"))
    return jax.shard_map(on_device, mesh=mesh, in_specs=in_specs, out_specs=out_specs, check_vma=False)
```
